32 devices in a mesh: freq: 2 (over x), sec: 16 (over z, y, core).
Axes of the slice: x: 2, y: 2, z: 4, core: 2. Of those that a mesh axis runs over, the one named last changes fastest.
Arguments:
- layer_trans: bfloat16 [16, 1024, 1024], P('sec'), may hold values from -0.1875 to 0.1875
- layer_refl: bfloat16 [16, 1024, 1024], P('sec'), may hold values from -0.046875 to 0.046875
- source_modes: int32 [256], P('freq'), parts along dimension 0, may hold values from 0 to 1023
Outputs:
- upgoing: bfloat16 [32, 64, 1024], P(('freq', 'sec')), parts along dimension 0
The draws below stay inside these ranges and needn't reach their ends.
There are 2 independent parts, one for each index of `freq`. The reference program is written for one: setup_inputs(seed, part) draws one part's arguments, and reference() takes and returns one part's arrays. A program takes and returns all parts, laid end to end along the dimension named above; an argument that names none is the same for every part. Nothing has to cross between parts.
All inputs are finite; a program needn't handle non-finite values.
Results may differ from the reference program's by a relative error of at most 0.035.
Values may be sent and summed in bfloat16 or wider, within the bound.
A program may use at most 64 MiB of HBM per device.

```python
import jax
import jax.numpy as jnp
from jax import lax

M = 1024
NSRC = 128
LAYERS = 16
N_SEC = 16


def touch_ends(entries, key, least, high):
    longest = entries.shape.index(max(entries.shape))
    spots = []
    for shift in (0, 1):
        where = [jax.random.randint(jax.random.fold_in(key, axis), (), 0, length) for axis, length in enumerate(entries.shape)]
        where[longest] = (where[longest] + shift) % entries.shape[longest]
        spots.append(tuple(where))
    return entries.at[spots[0]].set(least).at[spots[1]].set(high)


def levels(key, dims, pieces, low, largest):
    gain, own = 1.0, jax.random.fold_in(key, 6)
    for axis_at, shards_of in pieces:
        heights = jnp.exp(jax.random.uniform(jax.random.fold_in(own, axis_at), (shards_of,), jnp.float32, low / len(pieces), largest / len(pieces)))
        gain = gain * jnp.repeat(heights, dims[axis_at] // shards_of).reshape([-1 if axis == axis_at else 1 for axis in range(len(dims))])
    return gain


def gaussian(rng, shape, width, bound, shards=(), kind=jnp.bfloat16):
    drawn = jax.random.normal(rng, shape, jnp.float32) * width
    if len(shards) > 0:
        drawn = levels(rng, shape, shards, -0.22, 0.18) * drawn
    return jnp.clip(drawn, min=-bound, max=bound).astype(kind)


def setup_inputs(seed: int = 0, part: int = 0) -> dict:
    arg_keys = jax.random.split(jax.random.key(seed), 4)
    part_splits = jax.random.split(jax.random.fold_in(arg_keys[3], part), 4)
    return {
        "layer_trans": gaussian(arg_keys[0], (LAYERS, M, M), M ** -0.5, 0.1875, ((0, 16),)),
        "layer_refl": gaussian(arg_keys[1], (LAYERS, M, M), (M * LAYERS) ** -0.5, 0.046875, ((0, 16),)),
        "source_modes": touch_ends(jax.random.randint(part_splits[2], (NSRC,), 0, M), jax.random.fold_in(part_splits[2], 1), 0, M - 1).astype(jnp.int32),
    }


def reference(layer_trans, layer_refl, source_modes):
    def merge_pair(index):
        upper_t = lax.dynamic_index_in_dim(layer_trans, 2 * index, 0, keepdims=False).astype(jnp.float32)
        lower_t = lax.dynamic_index_in_dim(layer_trans, 2 * index + 1, 0, keepdims=False).astype(jnp.float32)
        upper_r = lax.dynamic_index_in_dim(layer_refl, 2 * index, 0, keepdims=False).astype(jnp.float32)
        lower_r = lax.dynamic_index_in_dim(layer_refl, 2 * index + 1, 0, keepdims=False).astype(jnp.float32)
        sect_t = jnp.dot(upper_t, lower_t, preferred_element_type=jnp.float32).astype(jnp.bfloat16)
        inner = jnp.dot(lower_r, upper_t.T, preferred_element_type=jnp.float32).astype(jnp.bfloat16)
        sect_r = (upper_r + jnp.dot(upper_t, inner.astype(jnp.float32), preferred_element_type=jnp.float32)).astype(jnp.bfloat16)
        return sect_t, sect_r

    sect_trans, sect_refl = lax.map(merge_pair, jnp.arange(N_SEC // 2, dtype=jnp.int32))
    down_first = (source_modes[:, None] == jnp.arange(M, dtype=jnp.int32)[None, :]).astype(jnp.bfloat16)

    def go_down(down, mats):
        sect_t, sect_r = mats
        down32 = down.astype(jnp.float32)
        echo = jnp.dot(down32, sect_r.astype(jnp.float32), preferred_element_type=jnp.float32)
        after = jnp.dot(down32, sect_t.astype(jnp.float32), preferred_element_type=jnp.float32).astype(jnp.bfloat16)
        return after, echo

    unused, echoes = lax.scan(go_down, down_first, (sect_trans, sect_refl))

    def go_up(upper, items):
        sect_t, echo = items
        value = (echo + jnp.dot(upper.astype(jnp.float32), sect_t.astype(jnp.float32).T, preferred_element_type=jnp.float32)).astype(jnp.bfloat16)
        return value, value

    start_up = jnp.zeros((NSRC, M), jnp.bfloat16)
    unused_up, ups = lax.scan(go_up, start_up, (sect_trans, echoes), reverse=True)
    return ups.reshape(N_SEC, NSRC // 2, M)
```

```python
import functools

import jax
import jax.numpy as jnp
from jax import lax
from jax.experimental import pallas as pl
from jax.experimental.pallas import tpu as pltpu
from jax.sharding import PartitionSpec as P

ROWS = 16
TILE = 256
F32 = jnp.float32
BF16 = jnp.bfloat16
MESH = pl.DeviceIdType.MESH


def nn(left, right):
    return jnp.dot(left, right, preferred_element_type=F32)


def nt(left, right):
    return lax.dot_general(left, right, (((1,), (1,)), ((), ())), preferred_element_type=F32)


def kernel(
    n, modes_ref, trans_ref, refl_ref, out_ref,
    trans, refl, merged, merged_t, inner, merged_r,
    down_in, down_out, up_in, echo,
    local_sem, pair_send, pair_recv, down_send, down_recv, up_send, up_recv,
):
    me = lax.axis_index("sec")
    section = me // 2
    parity = me % 2
    partner = me + 1 - 2 * parity
    sections = n // 2
    is_first = section == 0
    is_last = section == sections - 1
    below = lax.rem(me + 2, n)
    above = lax.rem(me + n - 2, n)
    modes = trans.shape[1]
    half = down_in.shape[0]
    batches = half // ROWS

    loads = []
    for which, (source, target) in enumerate(((trans_ref, trans), (refl_ref, refl))):
        loads.append(pltpu.make_async_copy(source.at[0], target.at[parity], local_sem.at[which]))
    for load in loads:
        load.start()

    barrier = pltpu.get_barrier_semaphore()

    def greet(device):
        pl.semaphore_signal(barrier, inc=1, device_id={"sec": device}, device_id_type=MESH)

    greet(partner)

    @pl.when(jnp.logical_not(is_first))
    def _():
        greet(above)

    @pl.when(jnp.logical_not(is_last))
    def _():
        greet(below)

    @pl.when(jnp.logical_or(is_first, is_last))
    def _():
        pl.semaphore_wait(barrier, 2)

    @pl.when(jnp.logical_not(jnp.logical_or(is_first, is_last)))
    def _():
        pl.semaphore_wait(barrier, 3)

    shares = []
    for which, (source, target) in enumerate(((trans_ref, trans), (refl_ref, refl))):
        shares.append(pltpu.make_async_remote_copy(
            src_ref=source.at[0], dst_ref=target.at[parity],
            send_sem=pair_send.at[which], recv_sem=pair_recv.at[which],
            device_id={"sec": partner}, device_id_type=MESH,
        ))
    for share in shares:
        share.start()

    def batch_rows(batch):
        return pl.ds(pl.multiple_of(batch * ROWS, ROWS), ROWS)

    def down_copy(batch):
        return pltpu.make_async_remote_copy(
            src_ref=down_out.at[batch_rows(batch), :], dst_ref=down_in.at[batch_rows(batch), :],
            send_sem=down_send.at[batch], recv_sem=down_recv.at[batch],
            device_id={"sec": below}, device_id_type=MESH,
        )

    def up_copy(batch):
        return pltpu.make_async_remote_copy(
            src_ref=out_ref.at[0, batch_rows(batch), :], dst_ref=up_in.at[batch_rows(batch), :],
            send_sem=up_send.at[batch], recv_sem=up_recv.at[batch],
            device_id={"sec": above}, device_id_type=MESH,
        )

    def merge_trans():
        def tile(step, carry):
            rows = pl.ds(pl.multiple_of(step * TILE, TILE), TILE)
            block = nn(trans[0, rows, :], trans[1]).astype(BF16)
            merged[rows, :] = block
            merged_t[:, rows] = block.T
            return carry

        lax.fori_loop(0, modes // TILE, tile, 0)

    loads[0].wait()
    shares[0].wait()

    @pl.when(is_first)
    def _():
        count = modes_ref.shape[1]
        row_at = lax.broadcasted_iota(jnp.int32, (count, count), 0)
        col_at = lax.broadcasted_iota(jnp.int32, (count, count), 1)
        spread = jnp.where(row_at == col_at, jnp.broadcast_to(modes_ref[...], (count, count)), 0)
        column = jnp.sum(spread, axis=1, keepdims=True)
        places = lax.broadcasted_iota(jnp.int32, (count, modes), 1)
        unit = (column == places).astype(F32).astype(BF16)
        for which in (0, 1):
            @pl.when(parity == which)
            def _():
                down_in[...] = unit[which * half:(which + 1) * half, :]

        def go(batch, carry):
            rows = batch_rows(batch)
            middle = nn(down_in[rows, :], trans[0]).astype(BF16)
            down_out[rows, :] = nn(middle, trans[1]).astype(BF16)
            down_copy(batch).start()
            return carry

        lax.fori_loop(0, batches, go, 0)
        merge_trans()

    @pl.when(jnp.logical_and(jnp.logical_not(is_first), jnp.logical_not(is_last)))
    def _():
        merge_trans()

        def go(batch, carry):
            rows = batch_rows(batch)
            down_copy(batch).wait_recv()
            down_out[rows, :] = nn(down_in[rows, :], merged[...]).astype(BF16)
            down_copy(batch).start()
            return carry

        lax.fori_loop(0, batches, go, 0)

    loads[1].wait()
    shares[1].wait()

    @pl.when(is_last)
    def _():
        def inner_tile(step, carry):
            rows = pl.ds(pl.multiple_of(step * TILE, TILE), TILE)
            inner[rows, :] = nt(refl[1, rows, :], trans[0]).astype(BF16)
            return carry

        lax.fori_loop(0, modes // TILE, inner_tile, 0)

        def refl_tile(step, carry):
            rows = pl.ds(pl.multiple_of(step * TILE, TILE), TILE)
            merged_r[rows, :] = (
                refl[0, rows, :].astype(F32) + nn(trans[0, rows, :], inner[...])
            ).astype(BF16)
            return carry

        lax.fori_loop(0, modes // TILE, refl_tile, 0)

        def go(batch, carry):
            rows = batch_rows(batch)
            down_copy(batch).wait_recv()
            out_ref[0, rows, :] = nn(down_in[rows, :], merged_r[...]).astype(BF16)
            up_copy(batch).start()
            return carry

        lax.fori_loop(0, batches, go, 0)

    @pl.when(jnp.logical_not(is_last))
    def _():
        field = down_in[...]
        middle = nn(field, trans[0]).astype(BF16)
        lower = nn(middle, refl[1]).astype(BF16)
        echo[...] = nn(field, refl[0]) + nt(lower, trans[0])

        def go(batch, carry):
            rows = batch_rows(batch)
            up_copy(batch).wait_recv()
            out_ref[0, rows, :] = (echo[rows, :] + nn(up_in[rows, :], merged_t[...])).astype(BF16)

            @pl.when(jnp.logical_not(is_first))
            def _():
                up_copy(batch).start()

            return carry

        lax.fori_loop(0, batches, go, 0)

        def sent(batch, carry):
            down_copy(batch).wait_send()
            return carry

        lax.fori_loop(0, batches, sent, 0)

    @pl.when(jnp.logical_not(is_first))
    def _():
        def sent(batch, carry):
            up_copy(batch).wait_send()
            return carry

        lax.fori_loop(0, batches, sent, 0)


def shards(n, layer_trans, layer_refl, source_modes):
    modes = layer_trans.shape[1]
    half = source_modes.shape[0] // 2
    batches = half // ROWS
    square = (modes, modes)
    vmem = pl.BlockSpec(memory_space=pltpu.VMEM)
    anywhere = pl.BlockSpec(memory_space=pl.ANY)
    return pl.pallas_call(
        functools.partial(kernel, n),
        out_shape=jax.ShapeDtypeStruct((1, half, modes), BF16),
        in_specs=[vmem, anywhere, anywhere],
        out_specs=vmem,
        scratch_shapes=[
            pltpu.VMEM((2, *square), BF16),
            pltpu.VMEM((2, *square), BF16),
            pltpu.VMEM(square, BF16),
            pltpu.VMEM(square, BF16),
            pltpu.VMEM(square, BF16),
            pltpu.VMEM(square, BF16),
            pltpu.VMEM((half, modes), BF16),
            pltpu.VMEM((half, modes), BF16),
            pltpu.VMEM((half, modes), BF16),
            pltpu.VMEM((half, modes), F32),
            pltpu.SemaphoreType.DMA((2,)),
            pltpu.SemaphoreType.DMA((2,)),
            pltpu.SemaphoreType.DMA((2,)),
            pltpu.SemaphoreType.DMA((batches,)),
            pltpu.SemaphoreType.DMA((batches,)),
            pltpu.SemaphoreType.DMA((batches,)),
            pltpu.SemaphoreType.DMA((batches,)),
        ],
        compiler_params=pltpu.CompilerParams(
            collective_id=0, has_side_effects=True, vmem_limit_bytes=56 * 1024 * 1024
        ),
    )(source_modes.reshape(1, -1), layer_trans, layer_refl)


def solution(mesh):
    return jax.shard_map(
        functools.partial(shards, mesh.shape["sec"]),
        mesh=mesh,
        in_specs=(P("sec", None, None), P("sec", None, None), P("freq")),
        out_specs=P(("freq", "sec"), None, None),
        check_vma=False,
    )
```

```python
import functools

import jax
import jax.numpy as jnp
from jax import lax
from jax.experimental import pallas as pl
from jax.experimental.pallas import tpu as pltpu
from jax.sharding import PartitionSpec as P

ROWS = 32
TILE = 256
F32 = jnp.float32
BF16 = jnp.bfloat16
MESH = pl.DeviceIdType.MESH


def nn(left, right):
    return jnp.dot(left, right, preferred_element_type=F32)


def each(count, body):
    def step(index, carry):
        body(index)
        return carry

    lax.fori_loop(0, count, step, 0)


def kernel(
    n, modes_ref, trans_ref, refl_ref, out_ref,
    upper_t, lower_t, upper_r, lower_r, merged, merged_t, inner,
    down_in, down_out, up_in, up_out, half_in, echo,
    local_sem, tile_send, tile_recv, pair_send, pair_recv, echo_sem,
    down_send, down_recv, pass_send, up_send, up_recv, half_send, half_recv,
):
    me = lax.axis_index("sec")
    section = me // 2
    parity = me % 2
    partner = me + 1 - 2 * parity
    sections = n // 2
    is_first = section == 0
    is_last = section == sections - 1
    not_first = jnp.logical_not(is_first)
    not_last = jnp.logical_not(is_last)
    on_zero = parity == 0
    on_one = parity == 1
    is_chain = jnp.logical_and(on_one, not_last)
    is_echo = jnp.logical_and(on_zero, not_last)
    is_turn = jnp.logical_and(on_zero, is_last)
    below = lax.rem(jnp.where(section == sections - 2, me + 1, me + 2), n)
    above = lax.rem(me + n - 1 - parity, n)
    modes = upper_t.shape[0]
    tiles = modes // TILE
    batches = down_in.shape[0] // ROWS
    half_batches = batches // 2
    half = half_in.shape[0]

    def tile_rows(tile):
        return pl.ds(pl.multiple_of(tile * TILE, TILE), TILE)

    def batch_rows(batch):
        return pl.ds(pl.multiple_of(batch * ROWS, ROWS), ROWS)

    def remote(source, target, send_sem, recv_sem, device):
        return pltpu.make_async_remote_copy(
            src_ref=source, dst_ref=target, send_sem=send_sem, recv_sem=recv_sem,
            device_id={"sec": device}, device_id_type=MESH,
        )

    load_t0 = pltpu.make_async_copy(trans_ref.at[0], upper_t, local_sem.at[0])
    load_t1 = pltpu.make_async_copy(trans_ref.at[0], lower_t, local_sem.at[0])
    load_r0 = pltpu.make_async_copy(refl_ref.at[0], upper_r, local_sem.at[1])

    @pl.when(on_zero)
    def _():
        load_t0.start()
        load_r0.start()

    @pl.when(on_one)
    def _():
        load_t1.start()

    barrier = pltpu.get_barrier_semaphore()

    def greet(device):
        pl.semaphore_signal(barrier, inc=1, device_id={"sec": device}, device_id_type=MESH)

    has_below = is_chain
    has_above = jnp.logical_or(is_turn, jnp.logical_and(is_chain, not_first))
    greet(partner)

    @pl.when(has_above)
    def _():
        greet(above)

    @pl.when(has_below)
    def _():
        greet(below)

    peers = 1 + has_above.astype(jnp.int32) + has_below.astype(jnp.int32)
    pl.semaphore_wait(barrier, peers)

    def tile_copy(tile):
        return remote(
            trans_ref.at[0, tile_rows(tile), :], upper_t.at[tile_rows(tile), :],
            tile_send.at[tile], tile_recv.at[tile], partner,
        )

    share_r = remote(refl_ref.at[0], lower_r, pair_send, pair_recv, partner)
    give_echo = remote(echo, echo, echo_sem.at[0], echo_sem.at[1], partner)

    def down_copy(batch):
        return remote(
            down_out.at[batch_rows(batch), :], down_in.at[batch_rows(batch), :],
            down_send.at[batch], down_recv.at[batch], below,
        )

    def middle_copy(batch):
        return remote(
            down_out.at[batch_rows(batch), :], down_in.at[batch_rows(batch), :],
            down_send.at[batch], down_recv.at[batch], partner,
        )

    def pass_copy(batch):
        return remote(
            down_in.at[batch_rows(batch), :], down_in.at[batch_rows(batch), :],
            pass_send.at[batch], down_recv.at[batch], partner,
        )

    def up_copy(batch):
        return remote(
            up_out.at[batch_rows(batch), :], up_in.at[batch_rows(batch), :],
            up_send.at[batch], up_recv.at[batch], above,
        )

    def half_copy(place):
        batch = (1 - parity) * half_batches + place
        return remote(
            up_out.at[batch_rows(batch), :], half_in.at[batch_rows(place), :],
            half_send.at[place], half_recv.at[place], partner,
        )

    def unit_rows():
        count = modes_ref.shape[1]
        row_at = lax.broadcasted_iota(jnp.int32, (count, count), 0)
        col_at = lax.broadcasted_iota(jnp.int32, (count, count), 1)
        spread = jnp.where(row_at == col_at, jnp.broadcast_to(modes_ref[...], (count, count)), 0)
        column = jnp.sum(spread, axis=1, keepdims=True)
        places = lax.broadcasted_iota(jnp.int32, (count, modes), 1)
        return (column == places).astype(F32).astype(BF16)

    def own_half():
        for which in (0, 1):
            @pl.when(parity == which)
            def _():
                out_ref[0] = up_out[which * half:(which + 1) * half, :]

    @pl.when(on_zero)
    def _():
        @pl.when(is_first)
        def _():
            down_in[...] = unit_rows()
            load_t0.wait()

            def go(batch):
                rows = batch_rows(batch)
                down_out[rows, :] = nn(down_in[rows, :], upper_t[...]).astype(BF16)
                middle_copy(batch).start()

            each(batches, go)

        each(tiles, lambda tile: tile_copy(tile).start())

        @pl.when(not_first)
        def _():
            load_t0.wait()

        def turn_tile(tile):
            merged_t[:, tile_rows(tile)] = upper_t[tile_rows(tile), :].T

        each(tiles, turn_tile)
        load_r0.wait()
        share_r.wait_recv()

        @pl.when(is_last)
        def _():
            def inner_tile(tile):
                rows = tile_rows(tile)
                inner[rows, :] = nn(lower_r[rows, :], merged_t[...]).astype(BF16)

            each(tiles, inner_tile)

            def refl_tile(tile):
                rows = tile_rows(tile)
                merged[rows, :] = (
                    upper_r[rows, :].astype(F32) + nn(upper_t[rows, :], inner[...])
                ).astype(BF16)

            each(tiles, refl_tile)

            def go(batch):
                rows = batch_rows(batch)
                down_copy(batch).wait_recv()
                up_out[rows, :] = nn(down_in[rows, :], merged[...]).astype(BF16)
                up_copy(batch).start()

            each(batches, go)
            each(half_batches, lambda place: half_copy(place).start())
            own_half()
            each(batches, lambda batch: up_copy(batch).wait_send())
            each(half_batches, lambda place: half_copy(place).wait_send())

        @pl.when(not_last)
        def _():
            @pl.when(not_first)
            def _():
                each(batches, lambda batch: pass_copy(batch).wait_recv())

            field = down_in[...]
            middle = nn(field, upper_t[...]).astype(BF16)
            lower = nn(middle, lower_r[...]).astype(BF16)
            echo[...] = nn(field, upper_r[...]) + nn(lower, merged_t[...])
            give_echo.start()

            @pl.when(is_first)
            def _():
                each(batches, lambda batch: middle_copy(batch).wait_send())

            each(half_batches, lambda place: half_copy(place).wait_recv())
            out_ref[0] = half_in[...]
            give_echo.wait_send()

        each(tiles, lambda tile: tile_copy(tile).wait_send())

    @pl.when(on_one)
    def _():
        share_r.start()
        load_t1.wait()

        @pl.when(is_first)
        def _():
            def go(batch):
                rows = batch_rows(batch)
                middle_copy(batch).wait_recv()
                down_out[rows, :] = nn(down_in[rows, :], lower_t[...]).astype(BF16)
                down_copy(batch).start()

            each(batches, go)

        @pl.when(section == 1)
        def _():
            each(tiles, lambda tile: tile_copy(tile).wait_recv())

        @pl.when(jnp.logical_and(section == 1, not_last))
        def _():
            def go(batch):
                rows = batch_rows(batch)
                down_copy(batch).wait_recv()
                middle = nn(down_in[rows, :], upper_t[...]).astype(BF16)
                down_out[rows, :] = nn(middle, lower_t[...]).astype(BF16)
                down_copy(batch).start()
                pass_copy(batch).start()

            each(batches, go)

        def merge_tile(tile):
            rows = tile_rows(tile)

            @pl.when(section != 1)
            def _():
                tile_copy(tile).wait_recv()

            block = nn(upper_t[rows, :], lower_t[...]).astype(BF16)
            merged[rows, :] = block
            merged_t[:, rows] = block.T

        each(tiles, merge_tile)

        @pl.when(jnp.logical_and(section > 1, not_last))
        def _():
            def go(batch):
                rows = batch_rows(batch)
                down_copy(batch).wait_recv()
                down_out[rows, :] = nn(down_in[rows, :], merged[...]).astype(BF16)
                down_copy(batch).start()
                pass_copy(batch).start()

            each(batches, go)

        @pl.when(not_last)
        def _():
            give_echo.wait_recv()

            def go(batch):
                rows = batch_rows(batch)
                up_copy(batch).wait_recv()
                up_out[rows, :] = (echo[rows, :] + nn(up_in[rows, :], merged_t[...])).astype(BF16)

                @pl.when(not_first)
                def _():
                    up_copy(batch).start()

                @pl.when(batch < half_batches)
                def _():
                    half_copy(batch).start()

            each(batches, go)
            own_half()
            each(batches, lambda batch: down_copy(batch).wait_send())
            each(half_batches, lambda place: half_copy(place).wait_send())

            @pl.when(not_first)
            def _():
                each(batches, lambda batch: up_copy(batch).wait_send())
                each(batches, lambda batch: pass_copy(batch).wait_send())

        @pl.when(is_last)
        def _():
            each(half_batches, lambda place: half_copy(place).wait_recv())
            out_ref[0] = half_in[...]

        share_r.wait_send()


def shards(n, layer_trans, layer_refl, source_modes):
    modes = layer_trans.shape[1]
    count = source_modes.shape[0]
    half = count // 2
    batches = count // ROWS
    square = (modes, modes)
    vmem = pl.BlockSpec(memory_space=pltpu.VMEM)
    anywhere = pl.BlockSpec(memory_space=pl.ANY)
    tiles = pltpu.SemaphoreType.DMA((modes // TILE,))
    per_batch = pltpu.SemaphoreType.DMA((batches,))
    per_half = pltpu.SemaphoreType.DMA((batches // 2,))
    return pl.pallas_call(
        functools.partial(kernel, n),
        out_shape=jax.ShapeDtypeStruct((1, half, modes), BF16),
        in_specs=[vmem, anywhere, anywhere],
        out_specs=vmem,
        scratch_shapes=[pltpu.VMEM(square, BF16)] * 7 + [
            pltpu.VMEM((count, modes), BF16),
            pltpu.VMEM((count, modes), BF16),
            pltpu.VMEM((count, modes), BF16),
            pltpu.VMEM((count, modes), BF16),
            pltpu.VMEM((half, modes), BF16),
            pltpu.VMEM((count, modes), F32),
            pltpu.SemaphoreType.DMA((2,)),
            tiles,
            tiles,
            pltpu.SemaphoreType.DMA,
            pltpu.SemaphoreType.DMA,
            pltpu.SemaphoreType.DMA((2,)),
            per_batch,
            per_batch,
            per_batch,
            per_batch,
            per_batch,
            per_half,
            per_half,
        ],
        compiler_params=pltpu.CompilerParams(
            collective_id=0, has_side_effects=True, vmem_limit_bytes=56 * 1024 * 1024
        ),
    )(source_modes.reshape(1, -1), layer_trans, layer_refl)


def solution(mesh):
    return jax.shard_map(
        functools.partial(shards, mesh.shape["sec"]),
        mesh=mesh,
        in_specs=(P("sec", None, None), P("sec", None, None), P("freq")),
        out_specs=P(("freq", "sec"), None, None),
        check_vma=False,
    )
```

```python
import functools

import jax
import jax.numpy as jnp
from jax import lax
from jax.experimental import pallas as pl
from jax.experimental.pallas import tpu as pltpu
from jax.sharding import PartitionSpec as P

ROWS = 32
TILE = 256
F32 = jnp.float32
BF16 = jnp.bfloat16
MESH = pl.DeviceIdType.MESH


def nn(left, right):
    return jnp.dot(left, right, preferred_element_type=F32)


def each(count, body):
    def step(index, carry):
        body(index)
        return carry

    lax.fori_loop(0, count, step, 0)


def kernel(
    n, modes_ref, trans_ref, refl_ref, out_ref,
    upper_t, lower_t, upper_r, lower_r, merged, merged_t, inner, odd_t, pair_t,
    down_in, down_out, up_in, up_out, odd_out, odd_echo, half_in, echo,
    local_sem, odd_send, odd_recv, odd_echo_sem, side_send, tile_send, tile_recv, pair_send, pair_recv, echo_sem,
    down_send, down_recv, pass_send, up_send, up_recv, half_send, half_recv,
):
    me = lax.axis_index("sec")
    section = me // 2
    parity = me % 2
    partner = me + 1 - 2 * parity
    sections = n // 2
    is_first = section == 0
    is_last = section == sections - 1
    not_first = jnp.logical_not(is_first)
    not_last = jnp.logical_not(is_last)
    on_zero = parity == 0
    on_one = parity == 1
    even = section % 2 == 0
    odd = section % 2 == 1
    paired = section < sections - 2
    below = lax.rem(jnp.where(section == sections - 2, me + 1, me + 2), n)
    above = lax.rem(me + n - 1 - 3 * parity, n)
    beside = lax.rem(me + n - 2, n)
    modes = upper_t.shape[0]
    tiles = modes // TILE
    batches = down_in.shape[0] // ROWS
    half_batches = batches // 2
    half = half_in.shape[0]

    def tile_rows(tile):
        return pl.ds(pl.multiple_of(tile * TILE, TILE), TILE)

    def batch_rows(batch):
        return pl.ds(pl.multiple_of(batch * ROWS, ROWS), ROWS)

    def remote(source, target, send_sem, recv_sem, device):
        return pltpu.make_async_remote_copy(
            src_ref=source, dst_ref=target, send_sem=send_sem, recv_sem=recv_sem,
            device_id={"sec": device}, device_id_type=MESH,
        )

    load_t0 = pltpu.make_async_copy(trans_ref.at[0], upper_t, local_sem.at[0])
    load_t1 = pltpu.make_async_copy(trans_ref.at[0], lower_t, local_sem.at[0])
    load_r0 = pltpu.make_async_copy(refl_ref.at[0], upper_r, local_sem.at[1])

    @pl.when(on_zero)
    def _():
        load_t0.start()
        load_r0.start()

    @pl.when(on_one)
    def _():
        load_t1.start()

    barrier = pltpu.get_barrier_semaphore()

    def greet(device):
        pl.semaphore_signal(barrier, inc=1, device_id={"sec": device}, device_id_type=MESH)

    greet(partner)
    zero_odd = jnp.logical_and(on_zero, odd)
    one_even = jnp.logical_and(on_one, even)
    one_odd = jnp.logical_and(jnp.logical_and(on_one, odd), not_last)
    even_paired = jnp.logical_and(one_even, paired)
    even_inside = jnp.logical_and(one_even, not_first)

    @pl.when(zero_odd)
    def _():
        greet(above)

    @pl.when(one_even)
    def _():
        greet(me + 1)

    @pl.when(even_paired)
    def _():
        greet(lax.rem(me + 2, n))
        greet(lax.rem(me + 4, n))

    @pl.when(even_inside)
    def _():
        greet(beside)
        greet(above)

    @pl.when(one_odd)
    def _():
        greet(beside)
        greet(lax.rem(me + 2, n))

    def number(flag):
        return flag.astype(jnp.int32)

    peers = (
        1 + number(zero_odd) + number(one_even)
        + 2 * (number(even_paired) + number(even_inside) + number(one_odd))
    )
    pl.semaphore_wait(barrier, peers)

    def tile_copy(tile):
        return remote(
            trans_ref.at[0, tile_rows(tile), :], upper_t.at[tile_rows(tile), :],
            tile_send.at[tile], tile_recv.at[tile], partner,
        )

    share_r = remote(refl_ref.at[0], lower_r, pair_send, pair_recv, partner)
    give_echo = remote(echo, echo, echo_sem.at[0], echo_sem.at[1], partner)

    def down_copy(batch):
        return remote(
            down_out.at[batch_rows(batch), :], down_in.at[batch_rows(batch), :],
            down_send.at[batch], down_recv.at[batch], below,
        )

    def middle_copy(batch):
        return remote(
            down_out.at[batch_rows(batch), :], down_in.at[batch_rows(batch), :],
            down_send.at[batch], down_recv.at[batch], partner,
        )

    def pass_copy(batch):
        return remote(
            down_in.at[batch_rows(batch), :], down_in.at[batch_rows(batch), :],
            pass_send.at[batch], down_recv.at[batch], partner,
        )

    def up_copy(batch):
        return remote(
            up_out.at[batch_rows(batch), :], up_in.at[batch_rows(batch), :],
            up_send.at[batch], up_recv.at[batch], above,
        )

    def side_copy(batch):
        return remote(
            up_out.at[batch_rows(batch), :], up_in.at[batch_rows(batch), :],
            side_send.at[batch], up_recv.at[batch], beside,
        )

    def odd_copy(tile):
        return remote(
            merged_t.at[tile_rows(tile), :], odd_t.at[tile_rows(tile), :],
            odd_send.at[tile], odd_recv.at[tile], beside,
        )

    odd_echo_copy = remote(odd_out, odd_echo, odd_echo_sem.at[0], odd_echo_sem.at[1], above)

    def half_copy(place):
        batch = (1 - parity) * half_batches + place
        return remote(
            up_out.at[batch_rows(batch), :], half_in.at[batch_rows(place), :],
            half_send.at[place], half_recv.at[place], partner,
        )

    def unit_rows():
        count = modes_ref.shape[1]
        row_at = lax.broadcasted_iota(jnp.int32, (count, count), 0)
        col_at = lax.broadcasted_iota(jnp.int32, (count, count), 1)
        spread = jnp.where(row_at == col_at, jnp.broadcast_to(modes_ref[...], (count, count)), 0)
        column = jnp.sum(spread, axis=1, keepdims=True)
        places = lax.broadcasted_iota(jnp.int32, (count, modes), 1)
        return (column == places).astype(F32).astype(BF16)

    def own_half():
        for which in (0, 1):
            @pl.when(parity == which)
            def _():
                out_ref[0] = up_out[which * half:(which + 1) * half, :]

    @pl.when(on_zero)
    def _():
        @pl.when(is_first)
        def _():
            down_in[...] = unit_rows()
            load_t0.wait()

            def go(batch):
                rows = batch_rows(batch)
                down_out[rows, :] = nn(down_in[rows, :], upper_t[...]).astype(BF16)
                middle_copy(batch).start()

            each(batches, go)

        each(tiles, lambda tile: tile_copy(tile).start())

        @pl.when(not_first)
        def _():
            load_t0.wait()

        def turn_tile(tile):
            merged_t[:, tile_rows(tile)] = upper_t[tile_rows(tile), :].T

        each(tiles, turn_tile)
        load_r0.wait()
        share_r.wait_recv()

        @pl.when(is_last)
        def _():
            def inner_tile(tile):
                rows = tile_rows(tile)
                inner[rows, :] = nn(lower_r[rows, :], merged_t[...]).astype(BF16)

            each(tiles, inner_tile)

            def refl_tile(tile):
                rows = tile_rows(tile)
                merged[rows, :] = (
                    upper_r[rows, :].astype(F32) + nn(upper_t[rows, :], inner[...])
                ).astype(BF16)

            each(tiles, refl_tile)

            def go(batch):
                rows = batch_rows(batch)
                down_copy(batch).wait_recv()
                up_out[rows, :] = nn(down_in[rows, :], merged[...]).astype(BF16)
                up_copy(batch).start()

            each(batches, go)
            each(half_batches, lambda place: half_copy(place).start())
            own_half()
            each(batches, lambda batch: up_copy(batch).wait_send())
            each(half_batches, lambda place: half_copy(place).wait_send())

        @pl.when(not_last)
        def _():
            @pl.when(not_first)
            def _():
                each(batches, lambda batch: pass_copy(batch).wait_recv())

            field = down_in[...]
            middle = nn(field, upper_t[...]).astype(BF16)
            lower = nn(middle, lower_r[...]).astype(BF16)
            value = nn(field, upper_r[...]) + nn(lower, merged_t[...])
            echo[...] = value
            odd_out[...] = value.astype(BF16)
            give_echo.start()

            @pl.when(odd)
            def _():
                odd_echo_copy.start()

            @pl.when(is_first)
            def _():
                each(batches, lambda batch: middle_copy(batch).wait_send())

            each(half_batches, lambda place: half_copy(place).wait_recv())
            out_ref[0] = half_in[...]
            give_echo.wait_send()

            @pl.when(odd)
            def _():
                odd_echo_copy.wait_send()

        each(tiles, lambda tile: tile_copy(tile).wait_send())

    @pl.when(on_one)
    def _():
        share_r.start()
        load_t1.wait()

        @pl.when(is_first)
        def _():
            def go(batch):
                rows = batch_rows(batch)
                middle_copy(batch).wait_recv()
                down_out[rows, :] = nn(down_in[rows, :], lower_t[...]).astype(BF16)
                down_copy(batch).start()

            each(batches, go)

        @pl.when(section == 1)
        def _():
            each(tiles, lambda tile: tile_copy(tile).wait_recv())

        @pl.when(jnp.logical_and(section == 1, not_last))
        def _():
            def go(batch):
                rows = batch_rows(batch)
                down_copy(batch).wait_recv()
                middle = nn(down_in[rows, :], upper_t[...]).astype(BF16)
                down_out[rows, :] = nn(middle, lower_t[...]).astype(BF16)
                down_copy(batch).start()
                pass_copy(batch).start()

            each(batches, go)

        def merge_tile(tile):
            rows = tile_rows(tile)

            @pl.when(section != 1)
            def _():
                tile_copy(tile).wait_recv()

            block = nn(upper_t[rows, :], lower_t[...]).astype(BF16)
            merged[rows, :] = block
            merged_t[:, rows] = block.T

        each(tiles, merge_tile)

        @pl.when(one_odd)
        def _():
            each(tiles, lambda tile: odd_copy(tile).start())

        @pl.when(jnp.logical_and(section > 1, not_last))
        def _():
            def go(batch):
                rows = batch_rows(batch)
                down_copy(batch).wait_recv()
                down_out[rows, :] = nn(down_in[rows, :], merged[...]).astype(BF16)
                down_copy(batch).start()
                pass_copy(batch).start()

            each(batches, go)

        @pl.when(not_last)
        def _():
            give_echo.wait_recv()

            @pl.when(even_paired)
            def _():
                odd_echo_copy.wait_recv()
                echo[...] += nn(odd_echo[...], merged_t[...])

                def pair_tile(tile):
                    rows = tile_rows(tile)
                    odd_copy(tile).wait_recv()
                    pair_t[rows, :] = nn(odd_t[rows, :], merged_t[...]).astype(BF16)

                each(tiles, pair_tile)

            def climb(step_t):
                def go(batch):
                    rows = batch_rows(batch)
                    up_copy(batch).wait_recv()
                    up_out[rows, :] = (echo[rows, :] + nn(up_in[rows, :], step_t[...])).astype(BF16)

                    @pl.when(even_inside)
                    def _():
                        up_copy(batch).start()
                        side_copy(batch).start()

                    @pl.when(batch < half_batches)
                    def _():
                        half_copy(batch).start()

                each(batches, go)

            @pl.when(even_paired)
            def _():
                climb(pair_t)

            @pl.when(jnp.logical_not(even_paired))
            def _():
                climb(merged_t)

            own_half()
            each(batches, lambda batch: down_copy(batch).wait_send())
            each(half_batches, lambda place: half_copy(place).wait_send())

            @pl.when(not_first)
            def _():
                each(batches, lambda batch: pass_copy(batch).wait_send())

            @pl.when(even_inside)
            def _():
                each(batches, lambda batch: up_copy(batch).wait_send())
                each(batches, lambda batch: side_copy(batch).wait_send())

            @pl.when(one_odd)
            def _():
                each(tiles, lambda tile: odd_copy(tile).wait_send())

        @pl.when(is_last)
        def _():
            each(half_batches, lambda place: half_copy(place).wait_recv())
            out_ref[0] = half_in[...]

        share_r.wait_send()


def shards(n, layer_trans, layer_refl, source_modes):
    modes = layer_trans.shape[1]
    count = source_modes.shape[0]
    half = count // 2
    batches = count // ROWS
    square = (modes, modes)
    vmem = pl.BlockSpec(memory_space=pltpu.VMEM)
    anywhere = pl.BlockSpec(memory_space=pl.ANY)
    tiles = pltpu.SemaphoreType.DMA((modes // TILE,))
    per_batch = pltpu.SemaphoreType.DMA((batches,))
    per_half = pltpu.SemaphoreType.DMA((batches // 2,))
    return pl.pallas_call(
        functools.partial(kernel, n),
        out_shape=jax.ShapeDtypeStruct((1, half, modes), BF16),
        in_specs=[vmem, anywhere, anywhere],
        out_specs=vmem,
        scratch_shapes=[pltpu.VMEM(square, BF16)] * 9 + [
            pltpu.VMEM((count, modes), BF16),
            pltpu.VMEM((count, modes), BF16),
            pltpu.VMEM((count, modes), BF16),
            pltpu.VMEM((count, modes), BF16),
            pltpu.VMEM((count, modes), BF16),
            pltpu.VMEM((count, modes), BF16),
            pltpu.VMEM((half, modes), BF16),
            pltpu.VMEM((count, modes), F32),
            pltpu.SemaphoreType.DMA((2,)),
            tiles,
            tiles,
            pltpu.SemaphoreType.DMA((2,)),
            per_batch,
            tiles,
            tiles,
            pltpu.SemaphoreType.DMA,
            pltpu.SemaphoreType.DMA,
            pltpu.SemaphoreType.DMA((2,)),
            per_batch,
            per_batch,
            per_batch,
            per_batch,
            per_batch,
            per_half,
            per_half,
        ],
        compiler_params=pltpu.CompilerParams(
            collective_id=0, has_side_effects=True, vmem_limit_bytes=56 * 1024 * 1024
        ),
    )(source_modes.reshape(1, -1), layer_trans, layer_refl)


def solution(mesh):
    return jax.shard_map(
        functools.partial(shards, mesh.shape["sec"]),
        mesh=mesh,
        in_specs=(P("sec", None, None), P("sec", None, None), P("freq")),
        out_specs=P(("freq", "sec"), None, None),
        check_vma=False,
    )
```

```python
import functools

import jax
import jax.numpy as jnp
from jax import lax
from jax.experimental import pallas as pl
from jax.experimental.pallas import tpu as pltpu
from jax.sharding import PartitionSpec as P

ROWS = 32
TILE = 256
F32 = jnp.float32
BF16 = jnp.bfloat16
MESH = pl.DeviceIdType.MESH


def nn(left, right):
    return jnp.dot(left, right, preferred_element_type=F32)


def each(count, body):
    def step(index, carry):
        body(index)
        return carry

    lax.fori_loop(0, count, step, 0)


def kernel(
    n, groups, modes_ref, trans_ref, refl_ref, out_ref,
    upper_t, lower_t, upper_r, lower_r, merged, merged_t, inner, odd_t, pair_t,
    down_in, down_out, up_in, up_out, odd_out, odd_echo, half_in, echo,
    local_sem, odd_send, odd_recv, odd_echo_sem, mate_send, mate_recv, side_send, tile_send, tile_recv, pair_send, pair_recv, echo_sem,
    down_send, down_recv, pass_send, up_send, up_recv, half_send, half_recv,
):
    me = lax.axis_index("sec")
    section = me // 2
    parity = me % 2
    partner = me + 1 - 2 * parity
    sections = n // 2
    is_first = section == 0
    is_last = section == sections - 1
    not_first = jnp.logical_not(is_first)
    not_last = jnp.logical_not(is_last)
    on_zero = parity == 0
    on_one = parity == 1
    shared = groups % 2 == 0
    group = lax.axis_index("freq")
    mate = group + 1 - 2 * (group % 2) if shared else group
    even = section % 2 == 0
    odd = section % 2 == 1
    paired = section < sections - 2
    below = lax.rem(jnp.where(section == sections - 2, me + 1, me + 2), n)
    above = lax.rem(me + n - 1 - 3 * parity, n)
    beside = lax.rem(me + n - 2, n)
    modes = upper_t.shape[0]
    tiles = modes // TILE
    own_tiles = tiles // 2 if shared else tiles
    first_own = (group % 2) * own_tiles if shared else 0
    first_other = own_tiles - first_own
    batches = down_in.shape[0] // ROWS
    half_batches = batches // 2
    half = half_in.shape[0]

    def tile_rows(tile):
        return pl.ds(pl.multiple_of(tile * TILE, TILE), TILE)

    def batch_rows(batch):
        return pl.ds(pl.multiple_of(batch * ROWS, ROWS), ROWS)

    def remote(source, target, send_sem, recv_sem, device):
        return pltpu.make_async_remote_copy(
            src_ref=source, dst_ref=target, send_sem=send_sem, recv_sem=recv_sem,
            device_id={"sec": device}, device_id_type=MESH,
        )

    load_t0 = pltpu.make_async_copy(trans_ref.at[0], upper_t, local_sem.at[0])
    load_t1 = pltpu.make_async_copy(trans_ref.at[0], lower_t, local_sem.at[0])
    load_r0 = pltpu.make_async_copy(refl_ref.at[0], upper_r, local_sem.at[1])

    @pl.when(on_zero)
    def _():
        load_t0.start()
        load_r0.start()

    @pl.when(on_one)
    def _():
        load_t1.start()

    barrier = pltpu.get_barrier_semaphore()

    def greet(device):
        pl.semaphore_signal(barrier, inc=1, device_id={"sec": device}, device_id_type=MESH)

    greet(partner)
    zero_odd = jnp.logical_and(on_zero, odd)
    one_even = jnp.logical_and(on_one, even)
    one_odd = jnp.logical_and(jnp.logical_and(on_one, odd), not_last)
    even_paired = jnp.logical_and(one_even, paired)
    even_inside = jnp.logical_and(one_even, not_first)

    @pl.when(zero_odd)
    def _():
        greet(above)

    @pl.when(one_even)
    def _():
        greet(me + 1)

    @pl.when(even_paired)
    def _():
        greet(lax.rem(me + 2, n))
        greet(lax.rem(me + 4, n))
        if shared:
            pl.semaphore_signal(
                barrier, inc=1, device_id={"freq": mate, "sec": me}, device_id_type=MESH
            )

    @pl.when(even_inside)
    def _():
        greet(beside)
        greet(above)

    @pl.when(one_odd)
    def _():
        greet(beside)
        greet(lax.rem(me + 2, n))

    def number(flag):
        return flag.astype(jnp.int32)

    peers = (
        1 + number(zero_odd) + number(one_even)
        + 2 * (number(even_inside) + number(one_odd)) + (3 if shared else 2) * number(even_paired)
    )
    pl.semaphore_wait(barrier, peers)

    def tile_copy(tile):
        return remote(
            trans_ref.at[0, tile_rows(tile), :], upper_t.at[tile_rows(tile), :],
            tile_send.at[tile], tile_recv.at[tile], partner,
        )

    share_r = remote(refl_ref.at[0], lower_r, pair_send, pair_recv, partner)
    give_echo = remote(echo, echo, echo_sem.at[0], echo_sem.at[1], partner)

    def down_copy(batch):
        return remote(
            down_out.at[batch_rows(batch), :], down_in.at[batch_rows(batch), :],
            down_send.at[batch], down_recv.at[batch], below,
        )

    def middle_copy(batch):
        return remote(
            down_out.at[batch_rows(batch), :], down_in.at[batch_rows(batch), :],
            down_send.at[batch], down_recv.at[batch], partner,
        )

    def pass_copy(batch):
        return remote(
            down_in.at[batch_rows(batch), :], down_in.at[batch_rows(batch), :],
            pass_send.at[batch], down_recv.at[batch], partner,
        )

    def up_copy(batch):
        return remote(
            up_out.at[batch_rows(batch), :], up_in.at[batch_rows(batch), :],
            up_send.at[batch], up_recv.at[batch], above,
        )

    def side_copy(batch):
        return remote(
            up_out.at[batch_rows(batch), :], up_in.at[batch_rows(batch), :],
            side_send.at[batch], up_recv.at[batch], beside,
        )

    def odd_copy(tile):
        return remote(
            merged_t.at[tile_rows(tile), :], odd_t.at[tile_rows(tile), :],
            odd_send.at[tile], odd_recv.at[tile], beside,
        )

    def mate_copy(tile):
        return pltpu.make_async_remote_copy(
            src_ref=pair_t.at[tile_rows(tile), :], dst_ref=pair_t.at[tile_rows(tile), :],
            send_sem=mate_send.at[tile], recv_sem=mate_recv.at[tile],
            device_id={"freq": mate, "sec": me}, device_id_type=MESH,
        )

    odd_echo_copy = remote(odd_out, odd_echo, odd_echo_sem.at[0], odd_echo_sem.at[1], above)

    def half_copy(place):
        batch = (1 - parity) * half_batches + place
        return remote(
            up_out.at[batch_rows(batch), :], half_in.at[batch_rows(place), :],
            half_send.at[place], half_recv.at[place], partner,
        )

    def unit_rows():
        count = modes_ref.shape[1]
        row_at = lax.broadcasted_iota(jnp.int32, (count, count), 0)
        col_at = lax.broadcasted_iota(jnp.int32, (count, count), 1)
        spread = jnp.where(row_at == col_at, jnp.broadcast_to(modes_ref[...], (count, count)), 0)
        column = jnp.sum(spread, axis=1, keepdims=True)
        places = lax.broadcasted_iota(jnp.int32, (count, modes), 1)
        return (column == places).astype(F32).astype(BF16)

    def own_half():
        for which in (0, 1):
            @pl.when(parity == which)
            def _():
                out_ref[0] = up_out[which * half:(which + 1) * half, :]

    @pl.when(on_zero)
    def _():
        @pl.when(is_first)
        def _():
            down_in[...] = unit_rows()
            load_t0.wait()

            def go(batch):
                rows = batch_rows(batch)
                down_out[rows, :] = nn(down_in[rows, :], upper_t[...]).astype(BF16)
                middle_copy(batch).start()

            each(batches, go)

        each(tiles, lambda tile: tile_copy(tile).start())

        @pl.when(not_first)
        def _():
            load_t0.wait()

        def turn_tile(tile):
            merged_t[:, tile_rows(tile)] = upper_t[tile_rows(tile), :].T

        each(tiles, turn_tile)
        load_r0.wait()
        share_r.wait_recv()

        @pl.when(is_last)
        def _():
            def inner_tile(tile):
                rows = tile_rows(tile)
                inner[rows, :] = nn(lower_r[rows, :], merged_t[...]).astype(BF16)

            each(tiles, inner_tile)

            def refl_tile(tile):
                rows = tile_rows(tile)
                merged[rows, :] = (
                    upper_r[rows, :].astype(F32) + nn(upper_t[rows, :], inner[...])
                ).astype(BF16)

            each(tiles, refl_tile)

            def go(batch):
                rows = batch_rows(batch)
                down_copy(batch).wait_recv()
                up_out[rows, :] = nn(down_in[rows, :], merged[...]).astype(BF16)
                up_copy(batch).start()

            each(batches, go)
            each(half_batches, lambda place: half_copy(place).start())
            own_half()
            each(batches, lambda batch: up_copy(batch).wait_send())
            each(half_batches, lambda place: half_copy(place).wait_send())

        @pl.when(not_last)
        def _():
            @pl.when(not_first)
            def _():
                each(batches, lambda batch: pass_copy(batch).wait_recv())

            field = down_in[...]
            middle = nn(field, upper_t[...]).astype(BF16)
            lower = nn(middle, lower_r[...]).astype(BF16)
            value = nn(field, upper_r[...]) + nn(lower, merged_t[...])
            echo[...] = value
            odd_out[...] = value.astype(BF16)
            give_echo.start()

            @pl.when(odd)
            def _():
                odd_echo_copy.start()

            @pl.when(is_first)
            def _():
                each(batches, lambda batch: middle_copy(batch).wait_send())

            each(half_batches, lambda place: half_copy(place).wait_recv())
            out_ref[0] = half_in[...]
            give_echo.wait_send()

            @pl.when(odd)
            def _():
                odd_echo_copy.wait_send()

        each(tiles, lambda tile: tile_copy(tile).wait_send())

    @pl.when(on_one)
    def _():
        share_r.start()
        load_t1.wait()

        @pl.when(is_first)
        def _():
            def go(batch):
                rows = batch_rows(batch)
                middle_copy(batch).wait_recv()
                down_out[rows, :] = nn(down_in[rows, :], lower_t[...]).astype(BF16)
                down_copy(batch).start()

            each(batches, go)

        @pl.when(section == 1)
        def _():
            each(tiles, lambda tile: tile_copy(tile).wait_recv())

        @pl.when(jnp.logical_and(section == 1, not_last))
        def _():
            def go(batch):
                rows = batch_rows(batch)
                down_copy(batch).wait_recv()
                middle = nn(down_in[rows, :], upper_t[...]).astype(BF16)
                down_out[rows, :] = nn(middle, lower_t[...]).astype(BF16)
                down_copy(batch).start()
                pass_copy(batch).start()

            each(batches, go)

        def merge_tile(tile):
            rows = tile_rows(tile)

            @pl.when(section != 1)
            def _():
                tile_copy(tile).wait_recv()

            block = nn(upper_t[rows, :], lower_t[...]).astype(BF16)
            merged[rows, :] = block
            merged_t[:, rows] = block.T

        each(tiles, merge_tile)

        @pl.when(one_odd)
        def _():
            each(own_tiles, lambda place: odd_copy(first_own + place).start())

        def pair_tile(place):
            tile = first_own + place
            rows = tile_rows(tile)
            odd_copy(tile).wait_recv()
            pair_t[rows, :] = nn(odd_t[rows, :], merged_t[...]).astype(BF16)
            if shared:
                mate_copy(tile).start()

        early = section >= 4

        @pl.when(jnp.logical_and(even_paired, early))
        def _():
            pair_tile(0)

        @pl.when(jnp.logical_and(section > 1, not_last))
        def _():
            def go(batch):
                rows = batch_rows(batch)
                down_copy(batch).wait_recv()
                down_out[rows, :] = nn(down_in[rows, :], merged[...]).astype(BF16)
                down_copy(batch).start()
                pass_copy(batch).start()

            each(batches, go)

        @pl.when(not_last)
        def _():
            @pl.when(jnp.logical_not(even_paired))
            def _():
                give_echo.wait_recv()

            @pl.when(even_paired)
            def _():
                @pl.when(jnp.logical_not(early))
                def _():
                    pair_tile(0)

                each(own_tiles - 1, lambda place: pair_tile(place + 1))
                give_echo.wait_recv()
                odd_echo_copy.wait_recv()
                echo[...] += nn(odd_echo[...], merged_t[...])
                if shared:
                    each(own_tiles, lambda place: mate_copy(first_other + place).wait_recv())

            def climb(step_t):
                def go(batch):
                    rows = batch_rows(batch)
                    up_copy(batch).wait_recv()
                    up_out[rows, :] = (echo[rows, :] + nn(up_in[rows, :], step_t[...])).astype(BF16)

                    @pl.when(even_inside)
                    def _():
                        up_copy(batch).start()
                        side_copy(batch).start()

                    @pl.when(batch < half_batches)
                    def _():
                        half_copy(batch).start()

                each(batches, go)

            @pl.when(even_paired)
            def _():
                climb(pair_t)

            @pl.when(jnp.logical_not(even_paired))
            def _():
                climb(merged_t)

            own_half()
            each(batches, lambda batch: down_copy(batch).wait_send())
            each(half_batches, lambda place: half_copy(place).wait_send())

            @pl.when(not_first)
            def _():
                each(batches, lambda batch: pass_copy(batch).wait_send())

            @pl.when(even_inside)
            def _():
                each(batches, lambda batch: up_copy(batch).wait_send())
                each(batches, lambda batch: side_copy(batch).wait_send())

            @pl.when(one_odd)
            def _():
                each(own_tiles, lambda place: odd_copy(first_own + place).wait_send())

            if shared:
                @pl.when(even_paired)
                def _():
                    each(own_tiles, lambda place: mate_copy(first_own + place).wait_send())

        @pl.when(is_last)
        def _():
            each(half_batches, lambda place: half_copy(place).wait_recv())
            out_ref[0] = half_in[...]

        share_r.wait_send()


def shards(n, groups, layer_trans, layer_refl, source_modes):
    modes = layer_trans.shape[1]
    count = source_modes.shape[0]
    half = count // 2
    batches = count // ROWS
    square = (modes, modes)
    vmem = pl.BlockSpec(memory_space=pltpu.VMEM)
    anywhere = pl.BlockSpec(memory_space=pl.ANY)
    tiles = pltpu.SemaphoreType.DMA((modes // TILE,))
    per_batch = pltpu.SemaphoreType.DMA((batches,))
    per_half = pltpu.SemaphoreType.DMA((batches // 2,))
    return pl.pallas_call(
        functools.partial(kernel, n, groups),
        out_shape=jax.ShapeDtypeStruct((1, half, modes), BF16),
        in_specs=[vmem, anywhere, anywhere],
        out_specs=vmem,
        scratch_shapes=[pltpu.VMEM(square, BF16)] * 9 + [
            pltpu.VMEM((count, modes), BF16),
            pltpu.VMEM((count, modes), BF16),
            pltpu.VMEM((count, modes), BF16),
            pltpu.VMEM((count, modes), BF16),
            pltpu.VMEM((count, modes), BF16),
            pltpu.VMEM((count, modes), BF16),
            pltpu.VMEM((half, modes), BF16),
            pltpu.VMEM((count, modes), F32),
            pltpu.SemaphoreType.DMA((2,)),
            tiles,
            tiles,
            pltpu.SemaphoreType.DMA((2,)),
            tiles,
            tiles,
            per_batch,
            tiles,
            tiles,
            pltpu.SemaphoreType.DMA,
            pltpu.SemaphoreType.DMA,
            pltpu.SemaphoreType.DMA((2,)),
            per_batch,
            per_batch,
            per_batch,
            per_batch,
            per_batch,
            per_half,
            per_half,
        ],
        compiler_params=pltpu.CompilerParams(
            collective_id=0, has_side_effects=True, vmem_limit_bytes=56 * 1024 * 1024
        ),
    )(source_modes.reshape(1, -1), layer_trans, layer_refl)


def solution(mesh):
    return jax.shard_map(
        functools.partial(shards, mesh.shape["sec"], mesh.shape["freq"]),
        mesh=mesh,
        in_specs=(P("sec", None, None), P("sec", None, None), P("freq")),
        out_specs=P(("freq", "sec"), None, None),
        check_vma=False,
    )
```

```python
import functools

import jax
import jax.numpy as jnp
from jax import lax
from jax.experimental import pallas as pl
from jax.experimental.pallas import tpu as pltpu
from jax.sharding import PartitionSpec as P

ROWS = 32
TILE = 256
PIECE = 128
F32 = jnp.float32
BF16 = jnp.bfloat16
MESH = pl.DeviceIdType.MESH


def nn(left, right):
    return jnp.dot(left, right, preferred_element_type=F32)


def each(count, body):
    def step(index, carry):
        body(index)
        return carry

    lax.fori_loop(0, count, step, 0)


def kernel(
    n, groups, modes_ref, trans_ref, refl_ref, out_ref,
    upper_t, lower_t, upper_r, lower_r, merged, merged_t, odd_t, pair_t,
    down_in, down_out, up_in, up_out, odd_out, odd_echo, half_in, echo,
    local_sem, odd_send, odd_recv, odd_echo_send, odd_echo_recv, piece_send, piece_recv, swap_send, swap_recv, mate_send, mate_recv, side_send, tile_send, tile_recv, pair_send, pair_recv, echo_send, echo_recv,
    down_send, down_recv, pass_send, up_send, up_recv, half_send, half_recv,
):
    me = lax.axis_index("sec")
    section = me // 2
    parity = me % 2
    partner = me + 1 - 2 * parity
    sections = n // 2
    is_first = section == 0
    is_last = section == sections - 1
    not_first = jnp.logical_not(is_first)
    not_last = jnp.logical_not(is_last)
    on_zero = parity == 0
    on_one = parity == 1
    shared = groups % 2 == 0
    group = lax.axis_index("freq")
    mate = group + 1 - 2 * (group % 2) if shared else group
    even = section % 2 == 0
    odd = section % 2 == 1
    paired = section < sections - 2
    is_turn = section == sections - 2
    below = lax.rem(jnp.where(section == sections - 2, me + 1, me + 2), n)
    above = lax.rem(me + n - 1 - 3 * parity, n)
    beside = lax.rem(me + n - 2, n)
    modes = upper_t.shape[0]
    tiles = modes // TILE
    own_tiles = tiles // 2 if shared else tiles
    first_own = (group % 2) * own_tiles if shared else 0
    first_other = own_tiles - first_own
    batches = down_in.shape[0] // ROWS
    half_batches = batches // 2
    half = half_in.shape[0]

    def tile_rows(tile):
        return pl.ds(pl.multiple_of(tile * TILE, TILE), TILE)

    def batch_rows(batch):
        return pl.ds(pl.multiple_of(batch * ROWS, ROWS), ROWS)

    def remote(source, target, send_sem, recv_sem, device):
        return pltpu.make_async_remote_copy(
            src_ref=source, dst_ref=target, send_sem=send_sem, recv_sem=recv_sem,
            device_id={"sec": device}, device_id_type=MESH,
        )

    load_t0 = pltpu.make_async_copy(trans_ref.at[0], upper_t, local_sem.at[0])
    load_t1 = pltpu.make_async_copy(trans_ref.at[0], lower_t, local_sem.at[0])
    load_r0 = pltpu.make_async_copy(refl_ref.at[0], upper_r, local_sem.at[1])

    @pl.when(on_zero)
    def _():
        load_t0.start()
        load_r0.start()

    @pl.when(on_one)
    def _():
        load_t1.start()

    barrier = pltpu.get_barrier_semaphore()

    def greet(device):
        pl.semaphore_signal(barrier, inc=1, device_id={"sec": device}, device_id_type=MESH)

    greet(partner)
    zero_odd = jnp.logical_and(on_zero, odd)
    one_even = jnp.logical_and(on_one, even)
    one_odd = jnp.logical_and(jnp.logical_and(on_one, odd), not_last)
    even_paired = jnp.logical_and(one_even, paired)
    even_inside = jnp.logical_and(one_even, not_first)

    @pl.when(zero_odd)
    def _():
        greet(above)

    @pl.when(one_even)
    def _():
        greet(me + 1)
        if shared:
            pl.semaphore_signal(
                barrier, inc=1, device_id={"freq": mate, "sec": me}, device_id_type=MESH
            )

    @pl.when(even_paired)
    def _():
        greet(lax.rem(me + 2, n))
        greet(lax.rem(me + 4, n))

    @pl.when(even_inside)
    def _():
        greet(beside)
        greet(above)

    @pl.when(one_odd)
    def _():
        greet(beside)
        greet(lax.rem(me + 2, n))

    def number(flag):
        return flag.astype(jnp.int32)

    peers = (
        1 + number(zero_odd) + (2 if shared else 1) * number(one_even)
        + 2 * (number(even_paired) + number(even_inside) + number(one_odd))
    )
    pl.semaphore_wait(barrier, peers)

    def tile_copy(tile):
        return remote(
            trans_ref.at[0, tile_rows(tile), :], upper_t.at[tile_rows(tile), :],
            tile_send.at[tile], tile_recv.at[tile], partner,
        )

    share_r = remote(refl_ref.at[0], lower_r, pair_send, pair_recv, partner)

    def down_copy(batch):
        return remote(
            down_out.at[batch_rows(batch), :], down_in.at[batch_rows(batch), :],
            down_send.at[batch], down_recv.at[batch], below,
        )

    def middle_copy(batch):
        return remote(
            down_out.at[batch_rows(batch), :], down_in.at[batch_rows(batch), :],
            down_send.at[batch], down_recv.at[batch], partner,
        )

    def pass_copy(batch):
        return remote(
            down_in.at[batch_rows(batch), :], down_in.at[batch_rows(batch), :],
            pass_send.at[batch], down_recv.at[batch], partner,
        )

    def up_copy(batch):
        return remote(
            up_out.at[batch_rows(batch), :], up_in.at[batch_rows(batch), :],
            up_send.at[batch], up_recv.at[batch], above,
        )

    def side_copy(batch):
        return remote(
            up_out.at[batch_rows(batch), :], up_in.at[batch_rows(batch), :],
            side_send.at[batch], up_recv.at[batch], beside,
        )

    def odd_copy(tile):
        return remote(
            merged_t.at[tile_rows(tile), :], odd_t.at[tile_rows(tile), :],
            odd_send.at[tile], odd_recv.at[tile], beside,
        )

    def mate_copy(tile):
        return pltpu.make_async_remote_copy(
            src_ref=pair_t.at[tile_rows(tile), :], dst_ref=pair_t.at[tile_rows(tile), :],
            send_sem=mate_send.at[tile], recv_sem=mate_recv.at[tile],
            device_id={"freq": mate, "sec": me}, device_id_type=MESH,
        )

    own_pieces = modes // PIECE // 2 if shared else modes // PIECE
    first_piece = (group % 2) * own_pieces if shared else 0
    other_piece = own_pieces - first_piece

    def piece_rows(piece):
        return pl.ds(pl.multiple_of(piece * PIECE, PIECE), PIECE)

    def piece_copy(piece):
        rows = piece_rows(piece)
        return remote(
            merged.at[rows, :], odd_t.at[rows, :], piece_send.at[piece], piece_recv.at[piece], above,
        )

    def swap_copy(piece):
        rows = piece_rows(piece)
        return pltpu.make_async_remote_copy(
            src_ref=odd_t.at[rows, :], dst_ref=odd_t.at[rows, :],
            send_sem=swap_send.at[piece], recv_sem=swap_recv.at[piece],
            device_id={"freq": mate, "sec": me}, device_id_type=MESH,
        )

    def echo_copy(batch):
        rows = batch_rows(batch)
        return remote(
            echo.at[rows, :], echo.at[rows, :], echo_send.at[batch], echo_recv.at[batch], partner,
        )

    def odd_echo_copy(batch):
        rows = batch_rows(batch)
        return remote(
            odd_out.at[rows, :], odd_echo.at[rows, :],
            odd_echo_send.at[batch], odd_echo_recv.at[batch], above,
        )

    def half_copy(place):
        batch = (1 - parity) * half_batches + place
        return remote(
            up_out.at[batch_rows(batch), :], half_in.at[batch_rows(place), :],
            half_send.at[place], half_recv.at[place], partner,
        )

    def unit_rows():
        count = modes_ref.shape[1]
        row_at = lax.broadcasted_iota(jnp.int32, (count, count), 0)
        col_at = lax.broadcasted_iota(jnp.int32, (count, count), 1)
        spread = jnp.where(row_at == col_at, jnp.broadcast_to(modes_ref[...], (count, count)), 0)
        column = jnp.sum(spread, axis=1, keepdims=True)
        places = lax.broadcasted_iota(jnp.int32, (count, modes), 1)
        return (column == places).astype(F32).astype(BF16)

    def own_half():
        for which in (0, 1):
            @pl.when(parity == which)
            def _():
                out_ref[0] = up_out[which * half:(which + 1) * half, :]

    @pl.when(on_zero)
    def _():
        @pl.when(is_first)
        def _():
            down_in[...] = unit_rows()
            load_t0.wait()

            def go(batch):
                rows = batch_rows(batch)
                down_out[rows, :] = nn(down_in[rows, :], upper_t[...]).astype(BF16)
                middle_copy(batch).start()

            each(batches, go)

        each(tiles, lambda tile: tile_copy(tile).start())

        @pl.when(not_first)
        def _():
            load_t0.wait()

        def turn_tile(tile):
            merged_t[:, tile_rows(tile)] = upper_t[tile_rows(tile), :].T

        each(tiles, turn_tile)
        load_r0.wait()
        share_r.wait_recv()

        def refl_tile(tile):
            rows = tile_rows(tile)
            half_way = nn(upper_t[rows, :], lower_r[...]).astype(BF16)
            merged[rows, :] = (
                upper_r[rows, :].astype(F32) + nn(half_way, merged_t[...])
            ).astype(BF16)

        def own_tile(place):
            tile = first_own + place
            refl_tile(tile)

            @pl.when(is_last)
            def _():
                each(TILE // PIECE, lambda part: piece_copy(tile * (TILE // PIECE) + part).start())

        each(own_tiles, own_tile)
        if shared:
            each(own_tiles, lambda place: refl_tile(first_other + place))

        def reflect(batch):
            rows = batch_rows(batch)

            @pl.when(not_first)
            def _():
                pass_copy(batch).wait_recv()

            value = nn(down_in[rows, :], merged[...])
            up_out[rows, :] = value.astype(BF16)

            @pl.when(not_last)
            def _():
                echo[rows, :] = value
                odd_out[rows, :] = value.astype(BF16)
                echo_copy(batch).start()

                @pl.when(odd)
                def _():
                    odd_echo_copy(batch).start()

            @pl.when(jnp.logical_and(is_last, batch >= half_batches))
            def _():
                half_copy(batch - half_batches).start()

        each(batches, reflect)

        @pl.when(is_last)
        def _():
            own_half()
            each(half_batches, lambda place: half_copy(place).wait_send())
            each(own_pieces, lambda place: piece_copy(first_piece + place).wait_send())

        @pl.when(not_last)
        def _():
            @pl.when(is_first)
            def _():
                each(batches, lambda batch: middle_copy(batch).wait_send())

            each(half_batches, lambda place: half_copy(place).wait_recv())
            out_ref[0] = half_in[...]
            each(batches, lambda batch: echo_copy(batch).wait_send())

            @pl.when(odd)
            def _():
                each(batches, lambda batch: odd_echo_copy(batch).wait_send())

        each(tiles, lambda tile: tile_copy(tile).wait_send())

    @pl.when(on_one)
    def _():
        share_r.start()
        load_t1.wait()

        @pl.when(is_first)
        def _():
            def go(batch):
                rows = batch_rows(batch)
                middle_copy(batch).wait_recv()
                down_out[rows, :] = nn(down_in[rows, :], lower_t[...]).astype(BF16)
                down_copy(batch).start()

            each(batches, go)

        @pl.when(section == 1)
        def _():
            each(tiles, lambda tile: tile_copy(tile).wait_recv())

        @pl.when(jnp.logical_and(section == 1, not_last))
        def _():
            def go(batch):
                rows = batch_rows(batch)
                down_copy(batch).wait_recv()
                middle = nn(down_in[rows, :], upper_t[...]).astype(BF16)
                down_out[rows, :] = nn(middle, lower_t[...]).astype(BF16)
                down_copy(batch).start()
                pass_copy(batch).start()

            each(batches, go)

        def merge_tile(tile):
            rows = tile_rows(tile)

            @pl.when(section != 1)
            def _():
                tile_copy(tile).wait_recv()

            block = nn(upper_t[rows, :], lower_t[...]).astype(BF16)
            merged[rows, :] = block
            merged_t[:, rows] = block.T

        each(tiles, merge_tile)

        @pl.when(one_odd)
        def _():
            each(own_tiles, lambda place: odd_copy(first_own + place).start())

        def pair_tile(place):
            tile = first_own + place
            rows = tile_rows(tile)
            odd_copy(tile).wait_recv()
            pair_t[rows, :] = nn(odd_t[rows, :], merged_t[...]).astype(BF16)
            if shared:
                mate_copy(tile).start()

        early = section >= 4

        @pl.when(jnp.logical_and(even_paired, early))
        def _():
            pair_tile(0)

        @pl.when(jnp.logical_and(on_one, is_turn))
        def _():
            def swap(place):
                piece = first_piece + place
                piece_copy(piece).wait_recv()
                if shared:
                    swap_copy(piece).start()

            each(own_pieces, swap)

        @pl.when(jnp.logical_and(section > 1, not_last))
        def _():
            def go(batch):
                rows = batch_rows(batch)
                down_copy(batch).wait_recv()

                @pl.when(is_turn)
                def _():
                    pass_copy(batch).start()

                down_out[rows, :] = nn(down_in[rows, :], merged[...]).astype(BF16)
                down_copy(batch).start()

                @pl.when(paired)
                def _():
                    pass_copy(batch).start()

                @pl.when(jnp.logical_and(odd, jnp.logical_not(paired)))
                def _():
                    pass_copy(batch).start()

            each(batches, go)

        @pl.when(not_last)
        def _():
            @pl.when(even_paired)
            def _():
                @pl.when(jnp.logical_not(early))
                def _():
                    pair_tile(0)

                each(own_tiles - 1, lambda place: pair_tile(place + 1))
                each(batches, lambda batch: echo_copy(batch).wait_recv())
                each(batches, lambda batch: odd_echo_copy(batch).wait_recv())
                echo[...] += nn(odd_echo[...], merged_t[...])
                if shared:
                    each(own_tiles, lambda place: mate_copy(first_other + place).wait_recv())

            @pl.when(is_turn)
            def _():
                if shared:
                    each(own_pieces, lambda place: swap_copy(other_piece + place).wait_recv())
                up_in[...] = nn(down_out[...], odd_t[...]).astype(BF16)

            def climb(step_t):
                def go(batch):
                    rows = batch_rows(batch)

                    @pl.when(jnp.logical_not(even_paired))
                    def _():
                        echo_copy(batch).wait_recv()

                    @pl.when(jnp.logical_not(is_turn))
                    def _():
                        up_copy(batch).wait_recv()

                    up_out[rows, :] = (echo[rows, :] + nn(up_in[rows, :], step_t[...])).astype(BF16)

                    @pl.when(even_inside)
                    def _():
                        up_copy(batch).start()
                        side_copy(batch).start()

                    @pl.when(batch < half_batches)
                    def _():
                        half_copy(batch).start()

                each(batches, go)

            @pl.when(even_paired)
            def _():
                climb(pair_t)

            @pl.when(jnp.logical_not(even_paired))
            def _():
                climb(merged_t)

            own_half()
            each(batches, lambda batch: down_copy(batch).wait_send())
            each(half_batches, lambda place: half_copy(place).wait_send())

            @pl.when(not_first)
            def _():
                each(batches, lambda batch: pass_copy(batch).wait_send())

            @pl.when(even_inside)
            def _():
                each(batches, lambda batch: up_copy(batch).wait_send())
                each(batches, lambda batch: side_copy(batch).wait_send())

            @pl.when(one_odd)
            def _():
                each(own_tiles, lambda place: odd_copy(first_own + place).wait_send())

            if shared:
                @pl.when(even_paired)
                def _():
                    each(own_tiles, lambda place: mate_copy(first_own + place).wait_send())

                @pl.when(is_turn)
                def _():
                    each(own_pieces, lambda place: swap_copy(first_piece + place).wait_send())

        @pl.when(is_last)
        def _():
            each(half_batches, lambda place: half_copy(place).wait_recv())
            out_ref[0] = half_in[...]

        share_r.wait_send()


def shards(n, groups, layer_trans, layer_refl, source_modes):
    modes = layer_trans.shape[1]
    count = source_modes.shape[0]
    half = count // 2
    batches = count // ROWS
    square = (modes, modes)
    vmem = pl.BlockSpec(memory_space=pltpu.VMEM)
    anywhere = pl.BlockSpec(memory_space=pl.ANY)
    tiles = pltpu.SemaphoreType.DMA((modes // TILE,))
    pieces = pltpu.SemaphoreType.DMA((modes // PIECE,))
    per_batch = pltpu.SemaphoreType.DMA((batches,))
    per_half = pltpu.SemaphoreType.DMA((batches // 2,))
    return pl.pallas_call(
        functools.partial(kernel, n, groups),
        out_shape=jax.ShapeDtypeStruct((1, half, modes), BF16),
        in_specs=[vmem, anywhere, anywhere],
        out_specs=vmem,
        scratch_shapes=[pltpu.VMEM(square, BF16)] * 8 + [
            pltpu.VMEM((count, modes), BF16),
            pltpu.VMEM((count, modes), BF16),
            pltpu.VMEM((count, modes), BF16),
            pltpu.VMEM((count, modes), BF16),
            pltpu.VMEM((count, modes), BF16),
            pltpu.VMEM((count, modes), BF16),
            pltpu.VMEM((half, modes), BF16),
            pltpu.VMEM((count, modes), F32),
            pltpu.SemaphoreType.DMA((2,)),
            tiles,
            tiles,
            per_batch,
            per_batch,
            pieces,
            pieces,
            pieces,
            pieces,
            tiles,
            tiles,
            per_batch,
            tiles,
            tiles,
            pltpu.SemaphoreType.DMA,
            pltpu.SemaphoreType.DMA,
            per_batch,
            per_batch,
            per_batch,
            per_batch,
            per_batch,
            per_batch,
            per_batch,
            per_half,
            per_half,
        ],
        compiler_params=pltpu.CompilerParams(
            collective_id=0, has_side_effects=True, vmem_limit_bytes=56 * 1024 * 1024
        ),
    )(source_modes.reshape(1, -1), layer_trans, layer_refl)


def solution(mesh):
    return jax.shard_map(
        functools.partial(shards, mesh.shape["sec"], mesh.shape["freq"]),
        mesh=mesh,
        in_specs=(P("sec", None, None), P("sec", None, None), P("freq")),
        out_specs=P(("freq", "sec"), None, None),
        check_vma=False,
    )
```

```python
import functools

import jax
import jax.numpy as jnp
from jax import lax
from jax.experimental import pallas as pl
from jax.experimental.pallas import tpu as pltpu
from jax.sharding import PartitionSpec as P

ROWS = 32
TILE = 256
PIECE = 128
F32 = jnp.float32
BF16 = jnp.bfloat16
MESH = pl.DeviceIdType.MESH


def nn(left, right):
    return jnp.dot(left, right, preferred_element_type=F32)


def each(count, body):
    def step(index, carry):
        body(index)
        return carry

    lax.fori_loop(0, count, step, 0)


def kernel(
    n, groups, modes_ref, trans_ref, refl_ref, out_ref,
    upper_t, lower_t, upper_r, lower_r, merged, merged_t, odd_t, pair_t,
    down_in, down_out, up_in, up_out, odd_out, odd_echo, half_in, echo,
    local_sem, odd_send, odd_recv, odd_echo_send, odd_echo_recv, piece_send, piece_recv, swap_send, swap_recv, mate_send, mate_recv, forward_send, side_send, tile_send, tile_recv, pair_send, pair_recv, echo_send, echo_recv,
    down_send, down_recv, pass_send, up_send, up_recv, half_send, half_recv,
):
    me = lax.axis_index("sec")
    section = me // 2
    parity = me % 2
    partner = me + 1 - 2 * parity
    sections = n // 2
    is_first = section == 0
    is_last = section == sections - 1
    not_first = jnp.logical_not(is_first)
    not_last = jnp.logical_not(is_last)
    on_zero = parity == 0
    on_one = parity == 1
    shared = groups % 2 == 0
    group = lax.axis_index("freq")
    mate = group + 1 - 2 * (group % 2) if shared else group
    even = section % 2 == 0
    odd = section % 2 == 1
    paired = section < sections - 2
    is_turn = section == sections - 2
    below = lax.rem(jnp.where(section == sections - 2, me + 1, me + 2), n)
    above = lax.rem(me + n - 1 - 3 * parity, n)
    beside = lax.rem(me + n - 2, n)
    modes = upper_t.shape[0]
    tiles = modes // TILE
    own_tiles = tiles // 2 if shared else tiles
    first_own = (group % 2) * own_tiles if shared else 0
    first_other = own_tiles - first_own
    batches = down_in.shape[0] // ROWS
    half_batches = batches // 2
    half = half_in.shape[0]

    def tile_rows(tile):
        return pl.ds(pl.multiple_of(tile * TILE, TILE), TILE)

    def batch_rows(batch):
        return pl.ds(pl.multiple_of(batch * ROWS, ROWS), ROWS)

    def remote(source, target, send_sem, recv_sem, device):
        return pltpu.make_async_remote_copy(
            src_ref=source, dst_ref=target, send_sem=send_sem, recv_sem=recv_sem,
            device_id={"sec": device}, device_id_type=MESH,
        )

    load_t0 = pltpu.make_async_copy(trans_ref.at[0], upper_t, local_sem.at[0])
    load_t1 = pltpu.make_async_copy(trans_ref.at[0], lower_t, local_sem.at[0])
    load_r0 = pltpu.make_async_copy(refl_ref.at[0], upper_r, local_sem.at[1])

    @pl.when(on_zero)
    def _():
        load_t0.start()
        load_r0.start()

    @pl.when(on_one)
    def _():
        load_t1.start()

    barrier = pltpu.get_barrier_semaphore()

    def greet(device):
        pl.semaphore_signal(barrier, inc=1, device_id={"sec": device}, device_id_type=MESH)

    greet(partner)
    zero_odd = jnp.logical_and(on_zero, odd)
    one_even = jnp.logical_and(on_one, even)
    one_odd = jnp.logical_and(jnp.logical_and(on_one, odd), not_last)
    even_paired = jnp.logical_and(one_even, paired)
    even_inside = jnp.logical_and(one_even, not_first)

    @pl.when(zero_odd)
    def _():
        greet(above)

    @pl.when(one_even)
    def _():
        greet(me + 1)
        if shared:
            pl.semaphore_signal(
                barrier, inc=1, device_id={"freq": mate, "sec": me}, device_id_type=MESH
            )

    @pl.when(even_paired)
    def _():
        greet(lax.rem(me + 2, n))
        greet(lax.rem(me + 4, n))

    @pl.when(even_inside)
    def _():
        greet(beside)
        greet(above)

    @pl.when(one_odd)
    def _():
        greet(beside)
        greet(lax.rem(me + 2, n))

    def number(flag):
        return flag.astype(jnp.int32)

    peers = (
        1 + number(zero_odd) + (2 if shared else 1) * number(one_even)
        + 2 * (number(even_paired) + number(even_inside) + number(one_odd))
    )
    pl.semaphore_wait(barrier, peers)

    def tile_copy(tile):
        return remote(
            trans_ref.at[0, tile_rows(tile), :], upper_t.at[tile_rows(tile), :],
            tile_send.at[tile], tile_recv.at[tile], partner,
        )

    share_r = remote(refl_ref.at[0], lower_r, pair_send, pair_recv, partner)

    def down_copy(batch):
        return remote(
            down_out.at[batch_rows(batch), :], down_in.at[batch_rows(batch), :],
            down_send.at[batch], down_recv.at[batch], below,
        )

    def middle_copy(batch):
        return remote(
            down_out.at[batch_rows(batch), :], down_in.at[batch_rows(batch), :],
            down_send.at[batch], down_recv.at[batch], partner,
        )

    def pass_copy(batch):
        return remote(
            down_in.at[batch_rows(batch), :], down_in.at[batch_rows(batch), :],
            pass_send.at[batch], down_recv.at[batch], partner,
        )

    def up_copy(batch):
        return remote(
            up_out.at[batch_rows(batch), :], up_in.at[batch_rows(batch), :],
            up_send.at[batch], up_recv.at[batch], above,
        )

    def side_copy(batch):
        return remote(
            up_out.at[batch_rows(batch), :], up_in.at[batch_rows(batch), :],
            side_send.at[batch], up_recv.at[batch], beside,
        )

    def forward_copy(batch):
        return remote(
            up_in.at[batch_rows(batch), :], up_in.at[batch_rows(batch), :],
            forward_send.at[batch], up_recv.at[batch], lax.rem(me + 2, n),
        )

    def odd_copy(tile):
        return remote(
            merged_t.at[tile_rows(tile), :], odd_t.at[tile_rows(tile), :],
            odd_send.at[tile], odd_recv.at[tile], beside,
        )

    def mate_copy(tile):
        return pltpu.make_async_remote_copy(
            src_ref=pair_t.at[tile_rows(tile), :], dst_ref=pair_t.at[tile_rows(tile), :],
            send_sem=mate_send.at[tile], recv_sem=mate_recv.at[tile],
            device_id={"freq": mate, "sec": me}, device_id_type=MESH,
        )

    own_pieces = modes // PIECE // 2 if shared else modes // PIECE
    first_piece = (group % 2) * own_pieces if shared else 0
    other_piece = own_pieces - first_piece

    def piece_rows(piece):
        return pl.ds(pl.multiple_of(piece * PIECE, PIECE), PIECE)

    def piece_copy(piece):
        rows = piece_rows(piece)
        return remote(
            merged.at[rows, :], odd_t.at[rows, :], piece_send.at[piece], piece_recv.at[piece], above,
        )

    def swap_copy(piece):
        rows = piece_rows(piece)
        return pltpu.make_async_remote_copy(
            src_ref=odd_t.at[rows, :], dst_ref=odd_t.at[rows, :],
            send_sem=swap_send.at[piece], recv_sem=swap_recv.at[piece],
            device_id={"freq": mate, "sec": me}, device_id_type=MESH,
        )

    def echo_copy(batch):
        rows = batch_rows(batch)
        return remote(
            echo.at[rows, :], echo.at[rows, :], echo_send.at[batch], echo_recv.at[batch], partner,
        )

    def odd_echo_copy(batch):
        rows = batch_rows(batch)
        return remote(
            odd_out.at[rows, :], odd_echo.at[rows, :],
            odd_echo_send.at[batch], odd_echo_recv.at[batch], above,
        )

    def half_copy(place):
        batch = (1 - parity) * half_batches + place
        return remote(
            up_out.at[batch_rows(batch), :], half_in.at[batch_rows(place), :],
            half_send.at[place], half_recv.at[place], partner,
        )

    def unit_rows():
        count = modes_ref.shape[1]
        row_at = lax.broadcasted_iota(jnp.int32, (count, count), 0)
        col_at = lax.broadcasted_iota(jnp.int32, (count, count), 1)
        spread = jnp.where(row_at == col_at, jnp.broadcast_to(modes_ref[...], (count, count)), 0)
        column = jnp.sum(spread, axis=1, keepdims=True)
        places = lax.broadcasted_iota(jnp.int32, (count, modes), 1)
        return (column == places).astype(F32).astype(BF16)

    def own_half():
        for which in (0, 1):
            @pl.when(parity == which)
            def _():
                out_ref[0] = up_out[which * half:(which + 1) * half, :]

    @pl.when(on_zero)
    def _():
        @pl.when(is_first)
        def _():
            down_in[...] = unit_rows()
            load_t0.wait()

            def go(batch):
                rows = batch_rows(batch)
                down_out[rows, :] = nn(down_in[rows, :], upper_t[...]).astype(BF16)
                middle_copy(batch).start()

            each(batches, go)

        each(tiles, lambda tile: tile_copy(tile).start())

        @pl.when(not_first)
        def _():
            load_t0.wait()

        def turn_tile(tile):
            merged_t[:, tile_rows(tile)] = upper_t[tile_rows(tile), :].T

        each(tiles, turn_tile)
        load_r0.wait()
        share_r.wait_recv()

        def refl_tile(tile):
            rows = tile_rows(tile)
            half_way = nn(upper_t[rows, :], lower_r[...]).astype(BF16)
            merged[rows, :] = (
                upper_r[rows, :].astype(F32) + nn(half_way, merged_t[...])
            ).astype(BF16)

        def own_tile(place):
            tile = first_own + place
            refl_tile(tile)

            @pl.when(is_last)
            def _():
                each(TILE // PIECE, lambda part: piece_copy(tile * (TILE // PIECE) + part).start())

        each(own_tiles, own_tile)
        if shared:
            each(own_tiles, lambda place: refl_tile(first_other + place))

        def reflect(batch):
            rows = batch_rows(batch)

            @pl.when(not_first)
            def _():
                pass_copy(batch).wait_recv()

            value = nn(down_in[rows, :], merged[...])
            up_out[rows, :] = value.astype(BF16)

            @pl.when(not_last)
            def _():
                echo[rows, :] = value
                odd_out[rows, :] = value.astype(BF16)
                echo_copy(batch).start()

                @pl.when(odd)
                def _():
                    odd_echo_copy(batch).start()

            @pl.when(jnp.logical_and(is_last, batch >= half_batches))
            def _():
                half_copy(batch - half_batches).start()

        each(batches, reflect)

        @pl.when(is_last)
        def _():
            own_half()
            each(half_batches, lambda place: half_copy(place).wait_send())
            each(own_pieces, lambda place: piece_copy(first_piece + place).wait_send())

        @pl.when(not_last)
        def _():
            @pl.when(is_first)
            def _():
                each(batches, lambda batch: middle_copy(batch).wait_send())

            each(half_batches, lambda place: half_copy(place).wait_recv())
            out_ref[0] = half_in[...]
            each(batches, lambda batch: echo_copy(batch).wait_send())

            @pl.when(odd)
            def _():
                each(batches, lambda batch: odd_echo_copy(batch).wait_send())

        each(tiles, lambda tile: tile_copy(tile).wait_send())

    @pl.when(on_one)
    def _():
        share_r.start()
        load_t1.wait()

        @pl.when(is_first)
        def _():
            def go(batch):
                rows = batch_rows(batch)
                middle_copy(batch).wait_recv()
                down_out[rows, :] = nn(down_in[rows, :], lower_t[...]).astype(BF16)
                down_copy(batch).start()

            each(batches, go)

        @pl.when(section == 1)
        def _():
            each(tiles, lambda tile: tile_copy(tile).wait_recv())

        @pl.when(jnp.logical_and(section == 1, not_last))
        def _():
            def go(batch):
                rows = batch_rows(batch)
                down_copy(batch).wait_recv()
                middle = nn(down_in[rows, :], upper_t[...]).astype(BF16)
                down_out[rows, :] = nn(middle, lower_t[...]).astype(BF16)
                down_copy(batch).start()
                pass_copy(batch).start()

            each(batches, go)

        def merge_tile(tile):
            rows = tile_rows(tile)

            @pl.when(section != 1)
            def _():
                tile_copy(tile).wait_recv()

            block = nn(upper_t[rows, :], lower_t[...]).astype(BF16)
            merged[rows, :] = block
            merged_t[:, rows] = block.T

        each(tiles, merge_tile)

        @pl.when(one_odd)
        def _():
            each(own_tiles, lambda place: odd_copy(first_own + place).start())

        def pair_tile(place):
            tile = first_own + place
            rows = tile_rows(tile)
            odd_copy(tile).wait_recv()
            pair_t[rows, :] = nn(odd_t[rows, :], merged_t[...]).astype(BF16)
            if shared:
                mate_copy(tile).start()

        early = section >= 4

        @pl.when(jnp.logical_and(even_paired, early))
        def _():
            pair_tile(0)

        @pl.when(jnp.logical_and(on_one, is_turn))
        def _():
            def swap(place):
                piece = first_piece + place
                piece_copy(piece).wait_recv()
                if shared:
                    swap_copy(piece).start()

            each(own_pieces, swap)

        @pl.when(jnp.logical_and(section > 1, not_last))
        def _():
            def go(batch):
                rows = batch_rows(batch)
                down_copy(batch).wait_recv()

                @pl.when(is_turn)
                def _():
                    pass_copy(batch).start()

                down_out[rows, :] = nn(down_in[rows, :], merged[...]).astype(BF16)
                down_copy(batch).start()

                @pl.when(paired)
                def _():
                    pass_copy(batch).start()

                @pl.when(jnp.logical_and(odd, jnp.logical_not(paired)))
                def _():
                    pass_copy(batch).start()

            each(batches, go)

        @pl.when(not_last)
        def _():
            @pl.when(even_paired)
            def _():
                @pl.when(jnp.logical_not(early))
                def _():
                    pair_tile(0)

                each(own_tiles - 1, lambda place: pair_tile(place + 1))
                each(batches, lambda batch: echo_copy(batch).wait_recv())
                each(batches, lambda batch: odd_echo_copy(batch).wait_recv())
                echo[...] += nn(odd_echo[...], merged_t[...])
                if shared:
                    each(own_tiles, lambda place: mate_copy(first_other + place).wait_recv())

            @pl.when(is_turn)
            def _():
                if shared:
                    each(own_pieces, lambda place: swap_copy(other_piece + place).wait_recv())
                up_in[...] = nn(down_out[...], odd_t[...]).astype(BF16)

            def climb(step_t):
                def go(batch):
                    rows = batch_rows(batch)

                    @pl.when(jnp.logical_not(even_paired))
                    def _():
                        echo_copy(batch).wait_recv()

                    @pl.when(jnp.logical_not(is_turn))
                    def _():
                        up_copy(batch).wait_recv()

                    @pl.when(jnp.logical_and(even_paired, batch < half_batches))
                    def _():
                        forward_copy(batch).start()

                    up_out[rows, :] = (echo[rows, :] + nn(up_in[rows, :], step_t[...])).astype(BF16)

                    @pl.when(even_inside)
                    def _():
                        up_copy(batch).start()

                    @pl.when(batch < half_batches)
                    def _():
                        half_copy(batch).start()

                each(batches, go)

                @pl.when(even_inside)
                def _():
                    each(half_batches, lambda place: side_copy(half_batches + place).start())

            @pl.when(even_paired)
            def _():
                climb(pair_t)

            @pl.when(jnp.logical_not(even_paired))
            def _():
                climb(merged_t)

            own_half()
            each(batches, lambda batch: down_copy(batch).wait_send())
            each(half_batches, lambda place: half_copy(place).wait_send())

            @pl.when(not_first)
            def _():
                each(batches, lambda batch: pass_copy(batch).wait_send())

            @pl.when(even_inside)
            def _():
                each(batches, lambda batch: up_copy(batch).wait_send())
                each(half_batches, lambda place: side_copy(half_batches + place).wait_send())

            @pl.when(even_paired)
            def _():
                each(half_batches, lambda batch: forward_copy(batch).wait_send())

            @pl.when(one_odd)
            def _():
                each(own_tiles, lambda place: odd_copy(first_own + place).wait_send())

            if shared:
                @pl.when(even_paired)
                def _():
                    each(own_tiles, lambda place: mate_copy(first_own + place).wait_send())

                @pl.when(is_turn)
                def _():
                    each(own_pieces, lambda place: swap_copy(first_piece + place).wait_send())

        @pl.when(is_last)
        def _():
            each(half_batches, lambda place: half_copy(place).wait_recv())
            out_ref[0] = half_in[...]

        share_r.wait_send()


def shards(n, groups, layer_trans, layer_refl, source_modes):
    modes = layer_trans.shape[1]
    count = source_modes.shape[0]
    half = count // 2
    batches = count // ROWS
    square = (modes, modes)
    vmem = pl.BlockSpec(memory_space=pltpu.VMEM)
    anywhere = pl.BlockSpec(memory_space=pl.ANY)
    tiles = pltpu.SemaphoreType.DMA((modes // TILE,))
    pieces = pltpu.SemaphoreType.DMA((modes // PIECE,))
    per_batch = pltpu.SemaphoreType.DMA((batches,))
    per_half = pltpu.SemaphoreType.DMA((batches // 2,))
    return pl.pallas_call(
        functools.partial(kernel, n, groups),
        out_shape=jax.ShapeDtypeStruct((1, half, modes), BF16),
        in_specs=[vmem, anywhere, anywhere],
        out_specs=vmem,
        scratch_shapes=[pltpu.VMEM(square, BF16)] * 8 + [
            pltpu.VMEM((count, modes), BF16),
            pltpu.VMEM((count, modes), BF16),
            pltpu.VMEM((count, modes), BF16),
            pltpu.VMEM((count, modes), BF16),
            pltpu.VMEM((count, modes), BF16),
            pltpu.VMEM((count, modes), BF16),
            pltpu.VMEM((half, modes), BF16),
            pltpu.VMEM((count, modes), F32),
            pltpu.SemaphoreType.DMA((2,)),
            tiles,
            tiles,
            per_batch,
            per_batch,
            pieces,
            pieces,
            pieces,
            pieces,
            tiles,
            tiles,
            per_half,
            per_batch,
            tiles,
            tiles,
            pltpu.SemaphoreType.DMA,
            pltpu.SemaphoreType.DMA,
            per_batch,
            per_batch,
            per_batch,
            per_batch,
            per_batch,
            per_batch,
            per_batch,
            per_half,
            per_half,
        ],
        compiler_params=pltpu.CompilerParams(
            collective_id=0, has_side_effects=True, vmem_limit_bytes=56 * 1024 * 1024
        ),
    )(source_modes.reshape(1, -1), layer_trans, layer_refl)


def solution(mesh):
    return jax.shard_map(
        functools.partial(shards, mesh.shape["sec"], mesh.shape["freq"]),
        mesh=mesh,
        in_specs=(P("sec", None, None), P("sec", None, None), P("freq")),
        out_specs=P(("freq", "sec"), None, None),
        check_vma=False,
    )
```

```python
import functools

import jax
import jax.numpy as jnp
from jax import lax
from jax.experimental import pallas as pl
from jax.experimental.pallas import tpu as pltpu
from jax.sharding import PartitionSpec as P

ROWS = 32
TILE = 256
PIECE = 128
F32 = jnp.float32
BF16 = jnp.bfloat16
MESH = pl.DeviceIdType.MESH


def nn(left, right):
    return jnp.dot(left, right, preferred_element_type=F32)


def each(count, body):
    def step(index, carry):
        body(index)
        return carry

    lax.fori_loop(0, count, step, 0)


def kernel(
    n, groups, modes_ref, trans_ref, refl_ref, out_ref,
    upper_t, lower_t, upper_r, lower_r, merged, merged_t, odd_t, pair_t,
    down_in, down_out, up_in, up_out, odd_out, odd_echo, half_in, echo,
    local_sem, odd_send, odd_recv, odd_echo_send, odd_echo_recv, piece_send, piece_recv, swap_send, swap_recv, mate_send, mate_recv, forward_send, side_send, tile_send, tile_recv, pair_send, pair_recv, echo_send, echo_recv,
    down_send, down_recv, pass_send, up_send, up_recv, half_send, half_recv,
):
    me = lax.axis_index("sec")
    section = me // 2
    parity = me % 2
    partner = me + 1 - 2 * parity
    sections = n // 2
    is_first = section == 0
    is_last = section == sections - 1
    not_first = jnp.logical_not(is_first)
    not_last = jnp.logical_not(is_last)
    on_zero = parity == 0
    on_one = parity == 1
    shared = groups % 2 == 0
    group = lax.axis_index("freq")
    mate = group + 1 - 2 * (group % 2) if shared else group
    even = section % 2 == 0
    odd = section % 2 == 1
    paired = section < sections - 2
    is_turn = section == sections - 2
    below = lax.rem(jnp.where(section == sections - 2, me + 1, me + 2), n)
    above = lax.rem(me + n - 1 - 3 * parity, n)
    beside = lax.rem(me + n - 2, n)
    modes = upper_t.shape[0]
    tiles = modes // TILE
    own_tiles = tiles // 2 if shared else tiles
    first_own = (group % 2) * own_tiles if shared else 0
    first_other = own_tiles - first_own
    batches = down_in.shape[0] // ROWS
    half_batches = batches // 2
    half = half_in.shape[0]

    def tile_rows(tile):
        return pl.ds(pl.multiple_of(tile * TILE, TILE), TILE)

    own_pieces = modes // PIECE // 2 if shared else modes // PIECE
    first_piece = (group % 2) * own_pieces if shared else 0
    other_piece = own_pieces - first_piece

    def piece_rows(piece):
        return pl.ds(pl.multiple_of(piece * PIECE, PIECE), PIECE)

    def batch_rows(batch):
        return pl.ds(pl.multiple_of(batch * ROWS, ROWS), ROWS)

    def remote(source, target, send_sem, recv_sem, device):
        return pltpu.make_async_remote_copy(
            src_ref=source, dst_ref=target, send_sem=send_sem, recv_sem=recv_sem,
            device_id={"sec": device}, device_id_type=MESH,
        )

    load_t0 = pltpu.make_async_copy(trans_ref.at[0], upper_t, local_sem.at[0])
    load_t1 = pltpu.make_async_copy(trans_ref.at[0], lower_t, local_sem.at[0])
    load_r0 = pltpu.make_async_copy(refl_ref.at[0], upper_r, local_sem.at[1])

    @pl.when(on_zero)
    def _():
        load_t0.start()
        load_r0.start()

    @pl.when(on_one)
    def _():
        load_t1.start()

    barrier = pltpu.get_barrier_semaphore()

    def greet(device):
        pl.semaphore_signal(barrier, inc=1, device_id={"sec": device}, device_id_type=MESH)

    greet(partner)
    zero_odd = jnp.logical_and(on_zero, odd)
    one_even = jnp.logical_and(on_one, even)
    one_odd = jnp.logical_and(jnp.logical_and(on_one, odd), not_last)
    even_paired = jnp.logical_and(one_even, paired)
    even_inside = jnp.logical_and(one_even, not_first)

    @pl.when(zero_odd)
    def _():
        greet(above)

    @pl.when(one_even)
    def _():
        greet(me + 1)
        if shared:
            pl.semaphore_signal(
                barrier, inc=1, device_id={"freq": mate, "sec": me}, device_id_type=MESH
            )

    @pl.when(even_paired)
    def _():
        greet(lax.rem(me + 2, n))
        greet(lax.rem(me + 4, n))

    @pl.when(even_inside)
    def _():
        greet(beside)
        greet(above)

    @pl.when(one_odd)
    def _():
        greet(beside)
        greet(lax.rem(me + 2, n))

    def number(flag):
        return flag.astype(jnp.int32)

    peers = (
        1 + number(zero_odd) + (2 if shared else 1) * number(one_even)
        + 2 * (number(even_paired) + number(even_inside) + number(one_odd))
    )
    pl.semaphore_wait(barrier, peers)

    def tile_copy(tile):
        return remote(
            trans_ref.at[0, tile_rows(tile), :], upper_t.at[tile_rows(tile), :],
            tile_send.at[tile], tile_recv.at[tile], partner,
        )

    share_r = remote(refl_ref.at[0], lower_r, pair_send, pair_recv, partner)

    def down_copy(batch):
        return remote(
            down_out.at[batch_rows(batch), :], down_in.at[batch_rows(batch), :],
            down_send.at[batch], down_recv.at[batch], below,
        )

    def middle_copy(batch):
        return remote(
            down_out.at[batch_rows(batch), :], down_in.at[batch_rows(batch), :],
            down_send.at[batch], down_recv.at[batch], partner,
        )

    def pass_copy(batch):
        return remote(
            down_in.at[batch_rows(batch), :], down_in.at[batch_rows(batch), :],
            pass_send.at[batch], down_recv.at[batch], partner,
        )

    def up_copy(batch):
        return remote(
            up_out.at[batch_rows(batch), :], up_in.at[batch_rows(batch), :],
            up_send.at[batch], up_recv.at[batch], above,
        )

    def side_copy(batch):
        return remote(
            up_out.at[batch_rows(batch), :], up_in.at[batch_rows(batch), :],
            side_send.at[batch], up_recv.at[batch], beside,
        )

    def forward_copy(batch):
        return remote(
            up_in.at[batch_rows(batch), :], up_in.at[batch_rows(batch), :],
            forward_send.at[batch], up_recv.at[batch], lax.rem(me + 2, n),
        )

    def odd_copy(piece):
        rows = piece_rows(piece)
        return remote(
            merged_t.at[rows, :], odd_t.at[rows, :], odd_send.at[piece], odd_recv.at[piece], beside,
        )

    def mate_copy(piece):
        rows = piece_rows(piece)
        return pltpu.make_async_remote_copy(
            src_ref=pair_t.at[rows, :], dst_ref=pair_t.at[rows, :],
            send_sem=mate_send.at[piece], recv_sem=mate_recv.at[piece],
            device_id={"freq": mate, "sec": me}, device_id_type=MESH,
        )

    def piece_copy(piece):
        rows = piece_rows(piece)
        return remote(
            merged.at[rows, :], odd_t.at[rows, :], piece_send.at[piece], piece_recv.at[piece], above,
        )

    def swap_copy(piece):
        rows = piece_rows(piece)
        return pltpu.make_async_remote_copy(
            src_ref=odd_t.at[rows, :], dst_ref=odd_t.at[rows, :],
            send_sem=swap_send.at[piece], recv_sem=swap_recv.at[piece],
            device_id={"freq": mate, "sec": me}, device_id_type=MESH,
        )

    def echo_copy(batch):
        rows = batch_rows(batch)
        return remote(
            echo.at[rows, :], echo.at[rows, :], echo_send.at[batch], echo_recv.at[batch], partner,
        )

    def odd_echo_copy(batch):
        rows = batch_rows(batch)
        return remote(
            odd_out.at[rows, :], odd_echo.at[rows, :],
            odd_echo_send.at[batch], odd_echo_recv.at[batch], above,
        )

    def half_copy(place):
        batch = (1 - parity) * half_batches + place
        return remote(
            up_out.at[batch_rows(batch), :], half_in.at[batch_rows(place), :],
            half_send.at[place], half_recv.at[place], partner,
        )

    def unit_rows():
        count = modes_ref.shape[1]
        row_at = lax.broadcasted_iota(jnp.int32, (count, count), 0)
        col_at = lax.broadcasted_iota(jnp.int32, (count, count), 1)
        spread = jnp.where(row_at == col_at, jnp.broadcast_to(modes_ref[...], (count, count)), 0)
        column = jnp.sum(spread, axis=1, keepdims=True)
        places = lax.broadcasted_iota(jnp.int32, (count, modes), 1)
        return (column == places).astype(F32).astype(BF16)

    def own_half():
        for which in (0, 1):
            @pl.when(parity == which)
            def _():
                out_ref[0] = up_out[which * half:(which + 1) * half, :]

    @pl.when(on_zero)
    def _():
        @pl.when(is_first)
        def _():
            down_in[...] = unit_rows()
            load_t0.wait()

            def go(batch):
                rows = batch_rows(batch)
                down_out[rows, :] = nn(down_in[rows, :], upper_t[...]).astype(BF16)
                middle_copy(batch).start()

            each(batches, go)

        each(tiles, lambda tile: tile_copy(tile).start())

        @pl.when(not_first)
        def _():
            load_t0.wait()

        def turn_tile(tile):
            merged_t[:, tile_rows(tile)] = upper_t[tile_rows(tile), :].T

        each(tiles, turn_tile)
        load_r0.wait()
        share_r.wait_recv()

        def refl_tile(tile):
            rows = tile_rows(tile)
            half_way = nn(upper_t[rows, :], lower_r[...]).astype(BF16)
            merged[rows, :] = (
                upper_r[rows, :].astype(F32) + nn(half_way, merged_t[...])
            ).astype(BF16)

        def own_tile(place):
            tile = first_own + place
            refl_tile(tile)

            @pl.when(is_last)
            def _():
                each(TILE // PIECE, lambda part: piece_copy(tile * (TILE // PIECE) + part).start())

        each(own_tiles, own_tile)
        if shared:
            each(own_tiles, lambda place: refl_tile(first_other + place))

        def reflect(batch):
            rows = batch_rows(batch)

            @pl.when(not_first)
            def _():
                pass_copy(batch).wait_recv()

            value = nn(down_in[rows, :], merged[...])
            up_out[rows, :] = value.astype(BF16)

            @pl.when(not_last)
            def _():
                echo[rows, :] = value
                odd_out[rows, :] = value.astype(BF16)
                echo_copy(batch).start()

                @pl.when(odd)
                def _():
                    odd_echo_copy(batch).start()

            @pl.when(jnp.logical_and(is_last, batch >= half_batches))
            def _():
                half_copy(batch - half_batches).start()

        each(batches, reflect)

        @pl.when(is_last)
        def _():
            own_half()
            each(half_batches, lambda place: half_copy(place).wait_send())
            each(own_pieces, lambda place: piece_copy(first_piece + place).wait_send())

        @pl.when(not_last)
        def _():
            @pl.when(is_first)
            def _():
                each(batches, lambda batch: middle_copy(batch).wait_send())

            each(half_batches, lambda place: half_copy(place).wait_recv())
            out_ref[0] = half_in[...]
            each(batches, lambda batch: echo_copy(batch).wait_send())

            @pl.when(odd)
            def _():
                each(batches, lambda batch: odd_echo_copy(batch).wait_send())

        each(tiles, lambda tile: tile_copy(tile).wait_send())

    @pl.when(on_one)
    def _():
        share_r.start()
        load_t1.wait()

        @pl.when(is_first)
        def _():
            def go(batch):
                rows = batch_rows(batch)
                middle_copy(batch).wait_recv()
                down_out[rows, :] = nn(down_in[rows, :], lower_t[...]).astype(BF16)
                down_copy(batch).start()

            each(batches, go)

        each(tiles, lambda tile: tile_copy(tile).wait_recv())

        @pl.when(jnp.logical_and(section == 1, not_last))
        def _():
            def go(batch):
                rows = batch_rows(batch)
                down_copy(batch).wait_recv()
                middle = nn(down_in[rows, :], upper_t[...]).astype(BF16)
                down_out[rows, :] = nn(middle, lower_t[...]).astype(BF16)
                down_copy(batch).start()
                pass_copy(batch).start()

            each(batches, go)

        def merge_tile(tile):
            columns = tile_rows(tile)
            block = nn(upper_t[...], lower_t[:, columns]).astype(BF16)
            merged[:, columns] = block
            merged_t[columns, :] = block.T

        def own_merge(place):
            tile = first_own + place
            merge_tile(tile)

            @pl.when(one_odd)
            def _():
                each(TILE // PIECE, lambda part: odd_copy(tile * (TILE // PIECE) + part).start())

        each(own_tiles, own_merge)
        if shared:
            each(own_tiles, lambda place: merge_tile(first_other + place))

        def pair_piece(place):
            piece = first_piece + place
            rows = piece_rows(piece)
            odd_copy(piece).wait_recv()
            pair_t[rows, :] = nn(odd_t[rows, :], merged_t[...]).astype(BF16)
            if shared:
                mate_copy(piece).start()

        early_pieces = own_pieces // 2
        early = section >= 4

        @pl.when(jnp.logical_and(even_paired, early))
        def _():
            each(early_pieces, pair_piece)

        @pl.when(jnp.logical_and(on_one, is_turn))
        def _():
            def swap(place):
                piece = first_piece + place
                piece_copy(piece).wait_recv()
                if shared:
                    swap_copy(piece).start()

            each(own_pieces, swap)

        @pl.when(jnp.logical_and(section > 1, not_last))
        def _():
            def go(batch):
                rows = batch_rows(batch)
                down_copy(batch).wait_recv()

                @pl.when(is_turn)
                def _():
                    pass_copy(batch).start()

                down_out[rows, :] = nn(down_in[rows, :], merged[...]).astype(BF16)
                down_copy(batch).start()

                @pl.when(paired)
                def _():
                    pass_copy(batch).start()

                @pl.when(jnp.logical_and(odd, jnp.logical_not(paired)))
                def _():
                    pass_copy(batch).start()

            each(batches, go)

        @pl.when(not_last)
        def _():
            @pl.when(even_paired)
            def _():
                @pl.when(jnp.logical_not(early))
                def _():
                    each(early_pieces, pair_piece)

                each(own_pieces - early_pieces, lambda place: pair_piece(early_pieces + place))
                each(batches, lambda batch: echo_copy(batch).wait_recv())
                each(batches, lambda batch: odd_echo_copy(batch).wait_recv())
                echo[...] += nn(odd_echo[...], merged_t[...])
                if shared:
                    each(own_pieces, lambda place: mate_copy(other_piece + place).wait_recv())

            @pl.when(is_turn)
            def _():
                if shared:
                    each(own_pieces, lambda place: swap_copy(other_piece + place).wait_recv())
                up_in[...] = nn(down_out[...], odd_t[...]).astype(BF16)

            def climb(step_t):
                def go(batch):
                    rows = batch_rows(batch)

                    @pl.when(jnp.logical_not(even_paired))
                    def _():
                        echo_copy(batch).wait_recv()

                    @pl.when(jnp.logical_not(is_turn))
                    def _():
                        up_copy(batch).wait_recv()

                    @pl.when(jnp.logical_and(even_paired, batch < half_batches))
                    def _():
                        forward_copy(batch).start()

                    up_out[rows, :] = (echo[rows, :] + nn(up_in[rows, :], step_t[...])).astype(BF16)

                    @pl.when(even_inside)
                    def _():
                        up_copy(batch).start()

                    @pl.when(batch < half_batches)
                    def _():
                        half_copy(batch).start()

                each(batches, go)

                @pl.when(even_inside)
                def _():
                    each(half_batches, lambda place: side_copy(half_batches + place).start())

            @pl.when(even_paired)
            def _():
                climb(pair_t)

            @pl.when(jnp.logical_not(even_paired))
            def _():
                climb(merged_t)

            own_half()
            each(batches, lambda batch: down_copy(batch).wait_send())
            each(half_batches, lambda place: half_copy(place).wait_send())

            @pl.when(not_first)
            def _():
                each(batches, lambda batch: pass_copy(batch).wait_send())

            @pl.when(even_inside)
            def _():
                each(batches, lambda batch: up_copy(batch).wait_send())
                each(half_batches, lambda place: side_copy(half_batches + place).wait_send())

            @pl.when(even_paired)
            def _():
                each(half_batches, lambda batch: forward_copy(batch).wait_send())

            @pl.when(one_odd)
            def _():
                each(own_pieces, lambda place: odd_copy(first_piece + place).wait_send())

            if shared:
                @pl.when(even_paired)
                def _():
                    each(own_pieces, lambda place: mate_copy(first_piece + place).wait_send())

                @pl.when(is_turn)
                def _():
                    each(own_pieces, lambda place: swap_copy(first_piece + place).wait_send())

        @pl.when(is_last)
        def _():
            each(half_batches, lambda place: half_copy(place).wait_recv())
            out_ref[0] = half_in[...]

        share_r.wait_send()


def shards(n, groups, layer_trans, layer_refl, source_modes):
    modes = layer_trans.shape[1]
    count = source_modes.shape[0]
    half = count // 2
    batches = count // ROWS
    square = (modes, modes)
    vmem = pl.BlockSpec(memory_space=pltpu.VMEM)
    anywhere = pl.BlockSpec(memory_space=pl.ANY)
    tiles = pltpu.SemaphoreType.DMA((modes // TILE,))
    pieces = pltpu.SemaphoreType.DMA((modes // PIECE,))
    per_batch = pltpu.SemaphoreType.DMA((batches,))
    per_half = pltpu.SemaphoreType.DMA((batches // 2,))
    return pl.pallas_call(
        functools.partial(kernel, n, groups),
        out_shape=jax.ShapeDtypeStruct((1, half, modes), BF16),
        in_specs=[vmem, anywhere, anywhere],
        out_specs=vmem,
        scratch_shapes=[pltpu.VMEM(square, BF16)] * 8 + [
            pltpu.VMEM((count, modes), BF16),
            pltpu.VMEM((count, modes), BF16),
            pltpu.VMEM((count, modes), BF16),
            pltpu.VMEM((count, modes), BF16),
            pltpu.VMEM((count, modes), BF16),
            pltpu.VMEM((count, modes), BF16),
            pltpu.VMEM((half, modes), BF16),
            pltpu.VMEM((count, modes), F32),
            pltpu.SemaphoreType.DMA((2,)),
            pieces,
            pieces,
            per_batch,
            per_batch,
            pieces,
            pieces,
            pieces,
            pieces,
            pieces,
            pieces,
            per_half,
            per_batch,
            tiles,
            tiles,
            pltpu.SemaphoreType.DMA,
            pltpu.SemaphoreType.DMA,
            per_batch,
            per_batch,
            per_batch,
            per_batch,
            per_batch,
            per_batch,
            per_batch,
            per_half,
            per_half,
        ],
        compiler_params=pltpu.CompilerParams(
            collective_id=0, has_side_effects=True, vmem_limit_bytes=56 * 1024 * 1024
        ),
    )(source_modes.reshape(1, -1), layer_trans, layer_refl)


def solution(mesh):
    return jax.shard_map(
        functools.partial(shards, mesh.shape["sec"], mesh.shape["freq"]),
        mesh=mesh,
        in_specs=(P("sec", None, None), P("sec", None, None), P("freq")),
        out_specs=P(("freq", "sec"), None, None),
        check_vma=False,
    )
```

```python
import functools

import jax
import jax.numpy as jnp
from jax import lax
from jax.experimental import pallas as pl
from jax.experimental.pallas import tpu as pltpu
from jax.sharding import PartitionSpec as P

ROWS = 32
TILE = 256
PIECE = 128
F32 = jnp.float32
BF16 = jnp.bfloat16
MESH = pl.DeviceIdType.MESH


def nn(left, right):
    return jnp.dot(left, right, preferred_element_type=F32)


def each(count, body):
    def step(index, carry):
        body(index)
        return carry

    lax.fori_loop(0, count, step, 0)


def kernel(
    n, groups, modes_ref, trans_ref, refl_ref, out_ref,
    upper_t, lower_t, upper_r, lower_r, merged, merged_t, odd_t, pair_t,
    down_in, down_out, up_in, up_out, odd_out, odd_echo, half_in, echo,
    local_sem, odd_send, odd_recv, odd_echo_send, odd_echo_recv, piece_send, piece_recv, swap_send, swap_recv, mate_send, mate_recv, forward_send, side_send, tile_send, tile_recv, pair_send, pair_recv, echo_send, echo_recv,
    down_send, down_recv, pass_send, up_send, up_recv, half_send, half_recv,
):
    me = lax.axis_index("sec")
    section = me // 2
    parity = me % 2
    partner = me + 1 - 2 * parity
    sections = n // 2
    is_first = section == 0
    is_last = section == sections - 1
    not_first = jnp.logical_not(is_first)
    not_last = jnp.logical_not(is_last)
    on_zero = parity == 0
    on_one = parity == 1
    shared = groups % 2 == 0
    group = lax.axis_index("freq")
    mate = group + 1 - 2 * (group % 2) if shared else group
    even = section % 2 == 0
    odd = section % 2 == 1
    paired = section < sections - 2
    is_turn = section == sections - 2
    below = lax.rem(jnp.where(section == sections - 2, me + 1, me + 2), n)
    above = lax.rem(me + n - 1 - 3 * parity, n)
    beside = lax.rem(me + n - 2, n)
    modes = upper_t.shape[0]
    tiles = modes // TILE
    own_tiles = tiles // 2 if shared else tiles
    first_own = (group % 2) * own_tiles if shared else 0
    first_other = own_tiles - first_own
    batches = down_in.shape[0] // ROWS
    half_batches = batches // 2
    half = half_in.shape[0]

    def tile_rows(tile):
        return pl.ds(pl.multiple_of(tile * TILE, TILE), TILE)

    own_pieces = modes // PIECE // 2 if shared else modes // PIECE
    first_piece = (group % 2) * own_pieces if shared else 0
    other_piece = own_pieces - first_piece

    def piece_rows(piece):
        return pl.ds(pl.multiple_of(piece * PIECE, PIECE), PIECE)

    def batch_rows(batch):
        return pl.ds(pl.multiple_of(batch * ROWS, ROWS), ROWS)

    def remote(source, target, send_sem, recv_sem, device):
        return pltpu.make_async_remote_copy(
            src_ref=source, dst_ref=target, send_sem=send_sem, recv_sem=recv_sem,
            device_id={"sec": device}, device_id_type=MESH,
        )

    load_t0 = pltpu.make_async_copy(trans_ref.at[0], upper_t, local_sem.at[0])
    load_t1 = pltpu.make_async_copy(trans_ref.at[0], lower_t, local_sem.at[0])
    load_r0 = pltpu.make_async_copy(refl_ref.at[0], upper_r, local_sem.at[1])

    @pl.when(on_zero)
    def _():
        load_t0.start()
        load_r0.start()

    @pl.when(on_one)
    def _():
        load_t1.start()

    barrier = pltpu.get_barrier_semaphore()

    def greet(device):
        pl.semaphore_signal(barrier, inc=1, device_id={"sec": device}, device_id_type=MESH)

    greet(partner)
    zero_odd = jnp.logical_and(on_zero, odd)
    one_even = jnp.logical_and(on_one, even)
    one_odd = jnp.logical_and(jnp.logical_and(on_one, odd), not_last)
    even_paired = jnp.logical_and(one_even, paired)
    even_inside = jnp.logical_and(one_even, not_first)

    @pl.when(zero_odd)
    def _():
        greet(above)

    @pl.when(one_even)
    def _():
        greet(me + 1)
        if shared:
            pl.semaphore_signal(
                barrier, inc=1, device_id={"freq": mate, "sec": me}, device_id_type=MESH
            )

    @pl.when(even_paired)
    def _():
        greet(lax.rem(me + 2, n))
        greet(lax.rem(me + 4, n))

    @pl.when(even_inside)
    def _():
        greet(beside)
        greet(above)

    @pl.when(one_odd)
    def _():
        greet(beside)
        greet(lax.rem(me + 2, n))

    def number(flag):
        return flag.astype(jnp.int32)

    peers = (
        1 + number(zero_odd) + (2 if shared else 1) * number(one_even)
        + 2 * (number(even_paired) + number(even_inside) + number(one_odd))
    )
    pl.semaphore_wait(barrier, peers)

    def tile_copy(tile):
        return remote(
            trans_ref.at[0, tile_rows(tile), :], upper_t.at[tile_rows(tile), :],
            tile_send.at[tile], tile_recv.at[tile], partner,
        )

    share_r = remote(refl_ref.at[0], lower_r, pair_send, pair_recv, partner)

    def down_copy(batch):
        return remote(
            down_out.at[batch_rows(batch), :], down_in.at[batch_rows(batch), :],
            down_send.at[batch], down_recv.at[batch], below,
        )

    def middle_copy(batch):
        return remote(
            down_out.at[batch_rows(batch), :], down_in.at[batch_rows(batch), :],
            down_send.at[batch], down_recv.at[batch], partner,
        )

    def pass_copy(batch):
        return remote(
            down_in.at[batch_rows(batch), :], down_in.at[batch_rows(batch), :],
            pass_send.at[batch], down_recv.at[batch], partner,
        )

    def up_copy(batch):
        return remote(
            up_out.at[batch_rows(batch), :], up_in.at[batch_rows(batch), :],
            up_send.at[batch], up_recv.at[batch], above,
        )

    def side_copy(batch):
        return remote(
            up_out.at[batch_rows(batch), :], up_in.at[batch_rows(batch), :],
            side_send.at[batch], up_recv.at[batch], beside,
        )

    def forward_copy(batch):
        return remote(
            up_in.at[batch_rows(batch), :], up_in.at[batch_rows(batch), :],
            forward_send.at[batch], up_recv.at[batch], lax.rem(me + 2, n),
        )

    def odd_copy(piece):
        rows = piece_rows(piece)
        return remote(
            merged_t.at[rows, :], odd_t.at[rows, :], odd_send.at[piece], odd_recv.at[piece], beside,
        )

    def mate_copy(piece):
        rows = piece_rows(piece)
        return pltpu.make_async_remote_copy(
            src_ref=pair_t.at[rows, :], dst_ref=pair_t.at[rows, :],
            send_sem=mate_send.at[piece], recv_sem=mate_recv.at[piece],
            device_id={"freq": mate, "sec": me}, device_id_type=MESH,
        )

    def piece_copy(piece):
        rows = piece_rows(piece)
        return remote(
            merged.at[rows, :], odd_t.at[rows, :], piece_send.at[piece], piece_recv.at[piece], above,
        )

    def swap_copy(piece):
        rows = piece_rows(piece)
        return pltpu.make_async_remote_copy(
            src_ref=odd_t.at[rows, :], dst_ref=odd_t.at[rows, :],
            send_sem=swap_send.at[piece], recv_sem=swap_recv.at[piece],
            device_id={"freq": mate, "sec": me}, device_id_type=MESH,
        )

    def echo_copy(batch):
        rows = batch_rows(batch)
        return remote(
            echo.at[rows, :], echo.at[rows, :], echo_send.at[batch], echo_recv.at[batch], partner,
        )

    def odd_echo_copy(batch):
        rows = batch_rows(batch)
        return remote(
            odd_out.at[rows, :], odd_echo.at[rows, :],
            odd_echo_send.at[batch], odd_echo_recv.at[batch], above,
        )

    def half_copy(place):
        batch = (1 - parity) * half_batches + place
        return remote(
            up_out.at[batch_rows(batch), :], half_in.at[batch_rows(place), :],
            half_send.at[place], half_recv.at[place], partner,
        )

    def unit_rows():
        count = modes_ref.shape[1]
        row_at = lax.broadcasted_iota(jnp.int32, (count, count), 0)
        col_at = lax.broadcasted_iota(jnp.int32, (count, count), 1)
        spread = jnp.where(row_at == col_at, jnp.broadcast_to(modes_ref[...], (count, count)), 0)
        column = jnp.sum(spread, axis=1, keepdims=True)
        places = lax.broadcasted_iota(jnp.int32, (count, modes), 1)
        return (column == places).astype(F32).astype(BF16)

    def own_half():
        for which in (0, 1):
            @pl.when(parity == which)
            def _():
                out_ref[0] = up_out[which * half:(which + 1) * half, :]

    @pl.when(on_zero)
    def _():
        @pl.when(is_first)
        def _():
            down_in[...] = unit_rows()
            load_t0.wait()

            def go(batch):
                rows = batch_rows(batch)
                down_out[rows, :] = nn(down_in[rows, :], upper_t[...]).astype(BF16)
                middle_copy(batch).start()

            each(batches, go)

        each(tiles, lambda tile: tile_copy(tile).start())

        @pl.when(not_first)
        def _():
            load_t0.wait()

        def turn_tile(tile):
            merged_t[:, tile_rows(tile)] = upper_t[tile_rows(tile), :].T

        each(tiles, turn_tile)
        load_r0.wait()
        share_r.wait_recv()

        def refl_tile(tile):
            rows = tile_rows(tile)
            half_way = nn(upper_t[rows, :], lower_r[...]).astype(BF16)
            merged[rows, :] = (
                upper_r[rows, :].astype(F32) + nn(half_way, merged_t[...])
            ).astype(BF16)

        def own_tile(place):
            tile = first_own + place
            refl_tile(tile)

            @pl.when(is_last)
            def _():
                each(TILE // PIECE, lambda part: piece_copy(tile * (TILE // PIECE) + part).start())

        each(own_tiles, own_tile)
        if shared:
            each(own_tiles, lambda place: refl_tile(first_other + place))

        def reflect(batch):
            rows = batch_rows(batch)

            @pl.when(not_first)
            def _():
                pass_copy(batch).wait_recv()

            value = nn(down_in[rows, :], merged[...])
            up_out[rows, :] = value.astype(BF16)

            @pl.when(not_last)
            def _():
                echo[rows, :] = value
                odd_out[rows, :] = value.astype(BF16)
                echo_copy(batch).start()

                @pl.when(odd)
                def _():
                    odd_echo_copy(batch).start()

            @pl.when(jnp.logical_and(is_last, batch >= half_batches))
            def _():
                half_copy(batch - half_batches).start()

        each(batches, reflect)

        @pl.when(is_last)
        def _():
            own_half()
            each(half_batches, lambda place: half_copy(place).wait_send())
            each(own_pieces, lambda place: piece_copy(first_piece + place).wait_send())

        @pl.when(not_last)
        def _():
            @pl.when(is_first)
            def _():
                each(batches, lambda batch: middle_copy(batch).wait_send())

            each(half_batches, lambda place: half_copy(place).wait_recv())
            out_ref[0] = half_in[...]
            each(batches, lambda batch: echo_copy(batch).wait_send())

            @pl.when(odd)
            def _():
                each(batches, lambda batch: odd_echo_copy(batch).wait_send())

        each(tiles, lambda tile: tile_copy(tile).wait_send())

    @pl.when(on_one)
    def _():
        share_r.start()
        load_t1.wait()

        @pl.when(is_first)
        def _():
            def go(batch):
                rows = batch_rows(batch)
                middle_copy(batch).wait_recv()
                down_out[rows, :] = nn(down_in[rows, :], lower_t[...]).astype(BF16)
                down_copy(batch).start()

            each(batches, go)

        each(tiles, lambda tile: tile_copy(tile).wait_recv())

        def merge_tile(tile):
            columns = tile_rows(tile)
            block = nn(upper_t[...], lower_t[:, columns]).astype(BF16)
            merged[:, columns] = block
            merged_t[columns, :] = block.T

        def own_merge(place):
            tile = first_own + place
            merge_tile(tile)

            @pl.when(one_odd)
            def _():
                each(TILE // PIECE, lambda part: odd_copy(tile * (TILE // PIECE) + part).start())

        each(own_tiles, own_merge)
        if shared:
            each(own_tiles, lambda place: merge_tile(first_other + place))

        def pair_piece(place):
            piece = first_piece + place
            rows = piece_rows(piece)
            odd_copy(piece).wait_recv()
            pair_t[rows, :] = nn(odd_t[rows, :], merged_t[...]).astype(BF16)
            if shared:
                mate_copy(piece).start()

        early_pieces = own_pieces // 2
        early = section >= 4

        @pl.when(jnp.logical_and(even_paired, early))
        def _():
            each(early_pieces, pair_piece)

        @pl.when(jnp.logical_and(on_one, is_turn))
        def _():
            def swap(place):
                piece = first_piece + place
                piece_copy(piece).wait_recv()
                if shared:
                    swap_copy(piece).start()

            each(own_pieces, swap)

        @pl.when(jnp.logical_and(not_first, not_last))
        def _():
            def go(batch):
                rows = batch_rows(batch)
                down_copy(batch).wait_recv()

                @pl.when(is_turn)
                def _():
                    pass_copy(batch).start()

                down_out[rows, :] = nn(down_in[rows, :], merged[...]).astype(BF16)
                down_copy(batch).start()

                @pl.when(paired)
                def _():
                    pass_copy(batch).start()

                @pl.when(jnp.logical_and(odd, jnp.logical_not(paired)))
                def _():
                    pass_copy(batch).start()

            each(batches, go)

        @pl.when(not_last)
        def _():
            @pl.when(even_paired)
            def _():
                @pl.when(jnp.logical_not(early))
                def _():
                    each(early_pieces, pair_piece)

                each(own_pieces - early_pieces, lambda place: pair_piece(early_pieces + place))
                each(batches, lambda batch: echo_copy(batch).wait_recv())
                each(batches, lambda batch: odd_echo_copy(batch).wait_recv())
                echo[...] += nn(odd_echo[...], merged_t[...])
                if shared:
                    each(own_pieces, lambda place: mate_copy(other_piece + place).wait_recv())

            @pl.when(is_turn)
            def _():
                if shared:
                    each(own_pieces, lambda place: swap_copy(other_piece + place).wait_recv())
                up_in[...] = nn(down_out[...], odd_t[...]).astype(BF16)

            def climb(step_t):
                def go(place):
                    in_turn = (place % 2) * half_batches + place // 2
                    batch = jnp.where(odd, in_turn, place)
                    rows = batch_rows(batch)

                    @pl.when(jnp.logical_not(even_paired))
                    def _():
                        echo_copy(batch).wait_recv()

                    @pl.when(jnp.logical_not(is_turn))
                    def _():
                        up_copy(batch).wait_recv()

                    @pl.when(jnp.logical_and(even_paired, batch < half_batches))
                    def _():
                        forward_copy(batch).start()

                    up_out[rows, :] = (echo[rows, :] + nn(up_in[rows, :], step_t[...])).astype(BF16)

                    @pl.when(even_inside)
                    def _():
                        up_copy(batch).start()

                    @pl.when(batch < half_batches)
                    def _():
                        half_copy(batch).start()

                each(batches, go)

                @pl.when(even_inside)
                def _():
                    each(half_batches, lambda place: side_copy(half_batches + place).start())

            @pl.when(even_paired)
            def _():
                climb(pair_t)

            @pl.when(jnp.logical_not(even_paired))
            def _():
                climb(merged_t)

            own_half()
            each(batches, lambda batch: down_copy(batch).wait_send())
            each(half_batches, lambda place: half_copy(place).wait_send())

            @pl.when(not_first)
            def _():
                each(batches, lambda batch: pass_copy(batch).wait_send())

            @pl.when(even_inside)
            def _():
                each(batches, lambda batch: up_copy(batch).wait_send())
                each(half_batches, lambda place: side_copy(half_batches + place).wait_send())

            @pl.when(even_paired)
            def _():
                each(half_batches, lambda batch: forward_copy(batch).wait_send())

            @pl.when(one_odd)
            def _():
                each(own_pieces, lambda place: odd_copy(first_piece + place).wait_send())

            if shared:
                @pl.when(even_paired)
                def _():
                    each(own_pieces, lambda place: mate_copy(first_piece + place).wait_send())

                @pl.when(is_turn)
                def _():
                    each(own_pieces, lambda place: swap_copy(first_piece + place).wait_send())

        @pl.when(is_last)
        def _():
            each(half_batches, lambda place: half_copy(place).wait_recv())
            out_ref[0] = half_in[...]

        share_r.wait_send()


def shards(n, groups, layer_trans, layer_refl, source_modes):
    modes = layer_trans.shape[1]
    count = source_modes.shape[0]
    half = count // 2
    batches = count // ROWS
    square = (modes, modes)
    vmem = pl.BlockSpec(memory_space=pltpu.VMEM)
    anywhere = pl.BlockSpec(memory_space=pl.ANY)
    tiles = pltpu.SemaphoreType.DMA((modes // TILE,))
    pieces = pltpu.SemaphoreType.DMA((modes // PIECE,))
    per_batch = pltpu.SemaphoreType.DMA((batches,))
    per_half = pltpu.SemaphoreType.DMA((batches // 2,))
    return pl.pallas_call(
        functools.partial(kernel, n, groups),
        out_shape=jax.ShapeDtypeStruct((1, half, modes), BF16),
        in_specs=[vmem, anywhere, anywhere],
        out_specs=vmem,
        scratch_shapes=[pltpu.VMEM(square, BF16)] * 8 + [
            pltpu.VMEM((count, modes), BF16),
            pltpu.VMEM((count, modes), BF16),
            pltpu.VMEM((count, modes), BF16),
            pltpu.VMEM((count, modes), BF16),
            pltpu.VMEM((count, modes), BF16),
            pltpu.VMEM((count, modes), BF16),
            pltpu.VMEM((half, modes), BF16),
            pltpu.VMEM((count, modes), F32),
            pltpu.SemaphoreType.DMA((2,)),
            pieces,
            pieces,
            per_batch,
            per_batch,
            pieces,
            pieces,
            pieces,
            pieces,
            pieces,
            pieces,
            per_half,
            per_batch,
            tiles,
            tiles,
            pltpu.SemaphoreType.DMA,
            pltpu.SemaphoreType.DMA,
            per_batch,
            per_batch,
            per_batch,
            per_batch,
            per_batch,
            per_batch,
            per_batch,
            per_half,
            per_half,
        ],
        compiler_params=pltpu.CompilerParams(
            collective_id=0, has_side_effects=True, vmem_limit_bytes=56 * 1024 * 1024
        ),
    )(source_modes.reshape(1, -1), layer_trans, layer_refl)


def solution(mesh):
    return jax.shard_map(
        functools.partial(shards, mesh.shape["sec"], mesh.shape["freq"]),
        mesh=mesh,
        in_specs=(P("sec", None, None), P("sec", None, None), P("freq")),
        out_specs=P(("freq", "sec"), None, None),
        check_vma=False,
    )
```

```python
import functools

import jax
import jax.numpy as jnp
from jax import lax
from jax.experimental import pallas as pl
from jax.experimental.pallas import tpu as pltpu
from jax.sharding import PartitionSpec as P

ROWS = 16
TILE = 256
PIECE = 128
F32 = jnp.float32
BF16 = jnp.bfloat16
MESH = pl.DeviceIdType.MESH


def nn(left, right):
    return jnp.dot(left, right, preferred_element_type=F32)


def each(count, body):
    def step(index, carry):
        body(index)
        return carry

    lax.fori_loop(0, count, step, 0)


def kernel(
    n, groups, modes_ref, trans_ref, refl_ref, out_ref,
    upper_t, lower_t, upper_r, lower_r, merged, merged_t, odd_t, pair_t,
    down_in, down_out, up_in, up_out, odd_out, odd_echo, half_in, echo,
    local_sem, odd_send, odd_recv, odd_echo_send, odd_echo_recv, piece_send, piece_recv, swap_send, swap_recv, mate_send, mate_recv, forward_send, side_send, tile_send, tile_recv, pair_send, pair_recv, echo_send, echo_recv,
    down_send, down_recv, pass_send, up_send, up_recv, half_send, half_recv,
):
    me = lax.axis_index("sec")
    section = me // 2
    parity = me % 2
    partner = me + 1 - 2 * parity
    sections = n // 2
    is_first = section == 0
    is_last = section == sections - 1
    not_first = jnp.logical_not(is_first)
    not_last = jnp.logical_not(is_last)
    on_zero = parity == 0
    on_one = parity == 1
    shared = groups % 2 == 0
    group = lax.axis_index("freq")
    mate = group + 1 - 2 * (group % 2) if shared else group
    even = section % 2 == 0
    odd = section % 2 == 1
    paired = section < sections - 2
    is_turn = section == sections - 2
    below = lax.rem(jnp.where(section == sections - 2, me + 1, me + 2), n)
    above = lax.rem(me + n - 1 - 3 * parity, n)
    beside = lax.rem(me + n - 2, n)
    modes = upper_t.shape[0]
    tiles = modes // TILE
    own_tiles = tiles // 2 if shared else tiles
    first_own = (group % 2) * own_tiles if shared else 0
    first_other = own_tiles - first_own
    batches = down_in.shape[0] // ROWS
    half_batches = batches // 2
    half = half_in.shape[0]

    def tile_rows(tile):
        return pl.ds(pl.multiple_of(tile * TILE, TILE), TILE)

    own_pieces = modes // PIECE // 2 if shared else modes // PIECE
    first_piece = (group % 2) * own_pieces if shared else 0
    other_piece = own_pieces - first_piece

    def piece_rows(piece):
        return pl.ds(pl.multiple_of(piece * PIECE, PIECE), PIECE)

    def batch_rows(batch):
        return pl.ds(pl.multiple_of(batch * ROWS, ROWS), ROWS)

    def remote(source, target, send_sem, recv_sem, device):
        return pltpu.make_async_remote_copy(
            src_ref=source, dst_ref=target, send_sem=send_sem, recv_sem=recv_sem,
            device_id={"sec": device}, device_id_type=MESH,
        )

    load_t0 = pltpu.make_async_copy(trans_ref.at[0], upper_t, local_sem.at[0])
    load_t1 = pltpu.make_async_copy(trans_ref.at[0], lower_t, local_sem.at[0])
    load_r0 = pltpu.make_async_copy(refl_ref.at[0], upper_r, local_sem.at[1])

    @pl.when(on_zero)
    def _():
        load_t0.start()
        load_r0.start()

    @pl.when(on_one)
    def _():
        load_t1.start()

    barrier = pltpu.get_barrier_semaphore()

    def greet(device):
        pl.semaphore_signal(barrier, inc=1, device_id={"sec": device}, device_id_type=MESH)

    greet(partner)
    zero_odd = jnp.logical_and(on_zero, odd)
    one_even = jnp.logical_and(on_one, even)
    one_odd = jnp.logical_and(jnp.logical_and(on_one, odd), not_last)
    even_paired = jnp.logical_and(one_even, paired)
    even_inside = jnp.logical_and(one_even, not_first)

    @pl.when(zero_odd)
    def _():
        greet(above)

    @pl.when(one_even)
    def _():
        greet(me + 1)
        if shared:
            pl.semaphore_signal(
                barrier, inc=1, device_id={"freq": mate, "sec": me}, device_id_type=MESH
            )

    @pl.when(even_paired)
    def _():
        greet(lax.rem(me + 2, n))
        greet(lax.rem(me + 4, n))

    @pl.when(even_inside)
    def _():
        greet(beside)
        greet(above)

    @pl.when(one_odd)
    def _():
        greet(beside)
        greet(lax.rem(me + 2, n))

    def number(flag):
        return flag.astype(jnp.int32)

    peers = (
        1 + number(zero_odd) + (2 if shared else 1) * number(one_even)
        + 2 * (number(even_paired) + number(even_inside) + number(one_odd))
    )
    pl.semaphore_wait(barrier, peers)

    def tile_copy(tile):
        return remote(
            trans_ref.at[0, tile_rows(tile), :], upper_t.at[tile_rows(tile), :],
            tile_send.at[tile], tile_recv.at[tile], partner,
        )

    share_r = remote(refl_ref.at[0], lower_r, pair_send, pair_recv, partner)

    def down_copy(batch):
        return remote(
            down_out.at[batch_rows(batch), :], down_in.at[batch_rows(batch), :],
            down_send.at[batch], down_recv.at[batch], below,
        )

    def middle_copy(batch):
        return remote(
            down_out.at[batch_rows(batch), :], down_in.at[batch_rows(batch), :],
            down_send.at[batch], down_recv.at[batch], partner,
        )

    def pass_copy(batch):
        return remote(
            down_in.at[batch_rows(batch), :], down_in.at[batch_rows(batch), :],
            pass_send.at[batch], down_recv.at[batch], partner,
        )

    def up_copy(batch):
        return remote(
            up_out.at[batch_rows(batch), :], up_in.at[batch_rows(batch), :],
            up_send.at[batch], up_recv.at[batch], above,
        )

    def side_copy(batch):
        return remote(
            up_out.at[batch_rows(batch), :], up_in.at[batch_rows(batch), :],
            side_send.at[batch], up_recv.at[batch], beside,
        )

    def forward_copy(batch):
        return remote(
            up_in.at[batch_rows(batch), :], up_in.at[batch_rows(batch), :],
            forward_send.at[batch], up_recv.at[batch], lax.rem(me + 2, n),
        )

    def odd_copy(piece):
        rows = piece_rows(piece)
        return remote(
            merged_t.at[rows, :], odd_t.at[rows, :], odd_send.at[piece], odd_recv.at[piece], beside,
        )

    def mate_copy(piece):
        rows = piece_rows(piece)
        return pltpu.make_async_remote_copy(
            src_ref=pair_t.at[rows, :], dst_ref=pair_t.at[rows, :],
            send_sem=mate_send.at[piece], recv_sem=mate_recv.at[piece],
            device_id={"freq": mate, "sec": me}, device_id_type=MESH,
        )

    def piece_copy(piece):
        rows = piece_rows(piece)
        return remote(
            merged.at[rows, :], odd_t.at[rows, :], piece_send.at[piece], piece_recv.at[piece], above,
        )

    def swap_copy(piece):
        rows = piece_rows(piece)
        return pltpu.make_async_remote_copy(
            src_ref=odd_t.at[rows, :], dst_ref=odd_t.at[rows, :],
            send_sem=swap_send.at[piece], recv_sem=swap_recv.at[piece],
            device_id={"freq": mate, "sec": me}, device_id_type=MESH,
        )

    def echo_copy(batch):
        rows = batch_rows(batch)
        return remote(
            echo.at[rows, :], echo.at[rows, :], echo_send.at[batch], echo_recv.at[batch], partner,
        )

    def odd_echo_copy(batch):
        rows = batch_rows(batch)
        return remote(
            odd_out.at[rows, :], odd_echo.at[rows, :],
            odd_echo_send.at[batch], odd_echo_recv.at[batch], above,
        )

    def half_copy(place):
        batch = (1 - parity) * half_batches + place
        return remote(
            up_out.at[batch_rows(batch), :], half_in.at[batch_rows(place), :],
            half_send.at[place], half_recv.at[place], partner,
        )

    def unit_rows():
        count = modes_ref.shape[1]
        row_at = lax.broadcasted_iota(jnp.int32, (count, count), 0)
        col_at = lax.broadcasted_iota(jnp.int32, (count, count), 1)
        spread = jnp.where(row_at == col_at, jnp.broadcast_to(modes_ref[...], (count, count)), 0)
        column = jnp.sum(spread, axis=1, keepdims=True)
        places = lax.broadcasted_iota(jnp.int32, (count, modes), 1)
        return (column == places).astype(F32).astype(BF16)

    def own_half():
        for which in (0, 1):
            @pl.when(parity == which)
            def _():
                out_ref[0] = up_out[which * half:(which + 1) * half, :]

    @pl.when(on_zero)
    def _():
        @pl.when(is_first)
        def _():
            down_in[...] = unit_rows()
            load_t0.wait()

            def go(batch):
                rows = batch_rows(batch)
                down_out[rows, :] = nn(down_in[rows, :], upper_t[...]).astype(BF16)
                middle_copy(batch).start()

            each(batches, go)

        each(tiles, lambda tile: tile_copy(tile).start())

        @pl.when(not_first)
        def _():
            load_t0.wait()

        def turn_tile(tile):
            merged_t[:, tile_rows(tile)] = upper_t[tile_rows(tile), :].T

        each(tiles, turn_tile)
        load_r0.wait()
        share_r.wait_recv()

        def refl_tile(tile):
            rows = tile_rows(tile)
            half_way = nn(upper_t[rows, :], lower_r[...]).astype(BF16)
            merged[rows, :] = (
                upper_r[rows, :].astype(F32) + nn(half_way, merged_t[...])
            ).astype(BF16)

        def own_tile(place):
            tile = first_own + place
            refl_tile(tile)

            @pl.when(is_last)
            def _():
                each(TILE // PIECE, lambda part: piece_copy(tile * (TILE // PIECE) + part).start())

        each(own_tiles, own_tile)
        if shared:
            each(own_tiles, lambda place: refl_tile(first_other + place))

        def reflect(batch):
            rows = batch_rows(batch)

            @pl.when(not_first)
            def _():
                pass_copy(batch).wait_recv()

            value = nn(down_in[rows, :], merged[...])
            up_out[rows, :] = value.astype(BF16)

            @pl.when(not_last)
            def _():
                echo[rows, :] = value
                odd_out[rows, :] = value.astype(BF16)
                echo_copy(batch).start()

                @pl.when(odd)
                def _():
                    odd_echo_copy(batch).start()

            @pl.when(jnp.logical_and(is_last, batch >= half_batches))
            def _():
                half_copy(batch - half_batches).start()

        each(batches, reflect)

        @pl.when(is_last)
        def _():
            own_half()
            each(half_batches, lambda place: half_copy(place).wait_send())
            each(own_pieces, lambda place: piece_copy(first_piece + place).wait_send())

        @pl.when(not_last)
        def _():
            @pl.when(is_first)
            def _():
                each(batches, lambda batch: middle_copy(batch).wait_send())

            each(half_batches, lambda place: half_copy(place).wait_recv())
            out_ref[0] = half_in[...]
            each(batches, lambda batch: echo_copy(batch).wait_send())

            @pl.when(odd)
            def _():
                each(batches, lambda batch: odd_echo_copy(batch).wait_send())

        each(tiles, lambda tile: tile_copy(tile).wait_send())

    @pl.when(on_one)
    def _():
        share_r.start()
        load_t1.wait()

        @pl.when(is_first)
        def _():
            def go(batch):
                rows = batch_rows(batch)
                middle_copy(batch).wait_recv()
                down_out[rows, :] = nn(down_in[rows, :], lower_t[...]).astype(BF16)
                down_copy(batch).start()

            each(batches, go)

        each(tiles, lambda tile: tile_copy(tile).wait_recv())

        def merge_tile(tile):
            columns = tile_rows(tile)
            block = nn(upper_t[...], lower_t[:, columns]).astype(BF16)
            merged[:, columns] = block
            merged_t[columns, :] = block.T

        def own_merge(place):
            tile = first_own + place
            merge_tile(tile)

            @pl.when(one_odd)
            def _():
                each(TILE // PIECE, lambda part: odd_copy(tile * (TILE // PIECE) + part).start())

        each(own_tiles, own_merge)
        if shared:
            each(own_tiles, lambda place: merge_tile(first_other + place))

        def pair_piece(place):
            piece = first_piece + place
            rows = piece_rows(piece)
            odd_copy(piece).wait_recv()
            pair_t[rows, :] = nn(odd_t[rows, :], merged_t[...]).astype(BF16)
            if shared:
                mate_copy(piece).start()

        early_pieces = own_pieces // 2
        early = section >= 4

        @pl.when(jnp.logical_and(even_paired, early))
        def _():
            each(early_pieces, pair_piece)

        @pl.when(jnp.logical_and(on_one, is_turn))
        def _():
            def swap(place):
                piece = first_piece + place
                piece_copy(piece).wait_recv()
                if shared:
                    swap_copy(piece).start()

            each(own_pieces, swap)

        @pl.when(jnp.logical_and(not_first, not_last))
        def _():
            def go(batch):
                rows = batch_rows(batch)
                down_copy(batch).wait_recv()

                @pl.when(is_turn)
                def _():
                    pass_copy(batch).start()

                down_out[rows, :] = nn(down_in[rows, :], merged[...]).astype(BF16)
                down_copy(batch).start()

                @pl.when(paired)
                def _():
                    pass_copy(batch).start()

                @pl.when(jnp.logical_and(odd, jnp.logical_not(paired)))
                def _():
                    pass_copy(batch).start()

            each(batches, go)

        @pl.when(not_last)
        def _():
            @pl.when(even_paired)
            def _():
                @pl.when(jnp.logical_not(early))
                def _():
                    each(early_pieces, pair_piece)

                each(own_pieces - early_pieces, lambda place: pair_piece(early_pieces + place))
                each(batches, lambda batch: echo_copy(batch).wait_recv())
                each(batches, lambda batch: odd_echo_copy(batch).wait_recv())
                echo[...] += nn(odd_echo[...], merged_t[...])
                if shared:
                    each(own_pieces, lambda place: mate_copy(other_piece + place).wait_recv())

            @pl.when(is_turn)
            def _():
                if shared:
                    each(own_pieces, lambda place: swap_copy(other_piece + place).wait_recv())
                up_in[...] = nn(down_out[...], odd_t[...]).astype(BF16)

            def climb(step_t):
                def go(place):
                    in_turn = (place % 2) * half_batches + place // 2
                    batch = jnp.where(odd, in_turn, place)
                    rows = batch_rows(batch)

                    @pl.when(jnp.logical_not(even_paired))
                    def _():
                        echo_copy(batch).wait_recv()

                    @pl.when(jnp.logical_not(is_turn))
                    def _():
                        up_copy(batch).wait_recv()

                    @pl.when(jnp.logical_and(even_paired, batch < half_batches))
                    def _():
                        forward_copy(batch).start()

                    up_out[rows, :] = (echo[rows, :] + nn(up_in[rows, :], step_t[...])).astype(BF16)

                    @pl.when(even_inside)
                    def _():
                        up_copy(batch).start()

                    @pl.when(batch < half_batches)
                    def _():
                        half_copy(batch).start()

                each(batches, go)

                @pl.when(even_inside)
                def _():
                    each(half_batches, lambda place: side_copy(half_batches + place).start())

            @pl.when(even_paired)
            def _():
                climb(pair_t)

            @pl.when(jnp.logical_not(even_paired))
            def _():
                climb(merged_t)

            own_half()
            each(batches, lambda batch: down_copy(batch).wait_send())
            each(half_batches, lambda place: half_copy(place).wait_send())

            @pl.when(not_first)
            def _():
                each(batches, lambda batch: pass_copy(batch).wait_send())

            @pl.when(even_inside)
            def _():
                each(batches, lambda batch: up_copy(batch).wait_send())
                each(half_batches, lambda place: side_copy(half_batches + place).wait_send())

            @pl.when(even_paired)
            def _():
                each(half_batches, lambda batch: forward_copy(batch).wait_send())

            @pl.when(one_odd)
            def _():
                each(own_pieces, lambda place: odd_copy(first_piece + place).wait_send())

            if shared:
                @pl.when(even_paired)
                def _():
                    each(own_pieces, lambda place: mate_copy(first_piece + place).wait_send())

                @pl.when(is_turn)
                def _():
                    each(own_pieces, lambda place: swap_copy(first_piece + place).wait_send())

        @pl.when(is_last)
        def _():
            each(half_batches, lambda place: half_copy(place).wait_recv())
            out_ref[0] = half_in[...]

        share_r.wait_send()


def shards(n, groups, layer_trans, layer_refl, source_modes):
    modes = layer_trans.shape[1]
    count = source_modes.shape[0]
    half = count // 2
    batches = count // ROWS
    square = (modes, modes)
    vmem = pl.BlockSpec(memory_space=pltpu.VMEM)
    anywhere = pl.BlockSpec(memory_space=pl.ANY)
    tiles = pltpu.SemaphoreType.DMA((modes // TILE,))
    pieces = pltpu.SemaphoreType.DMA((modes // PIECE,))
    per_batch = pltpu.SemaphoreType.DMA((batches,))
    per_half = pltpu.SemaphoreType.DMA((batches // 2,))
    return pl.pallas_call(
        functools.partial(kernel, n, groups),
        out_shape=jax.ShapeDtypeStruct((1, half, modes), BF16),
        in_specs=[vmem, anywhere, anywhere],
        out_specs=vmem,
        scratch_shapes=[pltpu.VMEM(square, BF16)] * 8 + [
            pltpu.VMEM((count, modes), BF16),
            pltpu.VMEM((count, modes), BF16),
            pltpu.VMEM((count, modes), BF16),
            pltpu.VMEM((count, modes), BF16),
            pltpu.VMEM((count, modes), BF16),
            pltpu.VMEM((count, modes), BF16),
            pltpu.VMEM((half, modes), BF16),
            pltpu.VMEM((count, modes), F32),
            pltpu.SemaphoreType.DMA((2,)),
            pieces,
            pieces,
            per_batch,
            per_batch,
            pieces,
            pieces,
            pieces,
            pieces,
            pieces,
            pieces,
            per_half,
            per_batch,
            tiles,
            tiles,
            pltpu.SemaphoreType.DMA,
            pltpu.SemaphoreType.DMA,
            per_batch,
            per_batch,
            per_batch,
            per_batch,
            per_batch,
            per_batch,
            per_batch,
            per_half,
            per_half,
        ],
        compiler_params=pltpu.CompilerParams(
            collective_id=0, has_side_effects=True, vmem_limit_bytes=56 * 1024 * 1024
        ),
    )(source_modes.reshape(1, -1), layer_trans, layer_refl)


def solution(mesh):
    return jax.shard_map(
        functools.partial(shards, mesh.shape["sec"], mesh.shape["freq"]),
        mesh=mesh,
        in_specs=(P("sec", None, None), P("sec", None, None), P("freq")),
        out_specs=P(("freq", "sec"), None, None),
        check_vma=False,
    )
```

```python
import functools

import jax
import jax.numpy as jnp
from jax import lax
from jax.experimental import pallas as pl
from jax.experimental.pallas import tpu as pltpu
from jax.sharding import PartitionSpec as P

ROWS = 16
TILE = 256
PIECE = 128
F32 = jnp.float32
BF16 = jnp.bfloat16
MESH = pl.DeviceIdType.MESH


def nn(left, right):
    return jnp.dot(left, right, preferred_element_type=F32)


def each(count, body):
    def step(index, carry):
        body(index)
        return carry

    lax.fori_loop(0, count, step, 0)


def kernel(
    n, groups, modes_ref, trans_ref, refl_ref, out_ref,
    upper_t, lower_t, upper_r, lower_r, merged, merged_t, odd_t, pair_t,
    down_in, down_out, up_in, up_out, odd_out, odd_echo, half_in, echo,
    local_sem, odd_send, odd_recv, odd_echo_send, odd_echo_recv, piece_send, piece_recv, swap_send, swap_recv, mate_send, mate_recv, forward_send, side_send, tile_send, tile_recv, pair_send, pair_recv, echo_send, echo_recv,
    down_send, down_recv, pass_send, up_send, up_recv, half_send, half_recv,
):
    me = lax.axis_index("sec")
    section = me // 2
    parity = me % 2
    partner = me + 1 - 2 * parity
    sections = n // 2
    is_first = section == 0
    is_last = section == sections - 1
    not_first = jnp.logical_not(is_first)
    not_last = jnp.logical_not(is_last)
    on_zero = parity == 0
    on_one = parity == 1
    shared = groups % 2 == 0
    group = lax.axis_index("freq")
    mate = group + 1 - 2 * (group % 2) if shared else group
    even = section % 2 == 0
    odd = section % 2 == 1
    paired = section < sections - 2
    is_turn = section == sections - 2
    below = lax.rem(jnp.where(section == sections - 2, me + 1, me + 2), n)
    above = lax.rem(me + n - 1 - 3 * parity, n)
    beside = lax.rem(me + n - 2, n)
    modes = upper_t.shape[0]
    tiles = modes // TILE
    own_tiles = tiles // 2 if shared else tiles
    first_own = (group % 2) * own_tiles if shared else 0
    first_other = own_tiles - first_own
    batches = down_in.shape[0] // ROWS
    half_batches = batches // 2
    half = half_in.shape[0]

    def tile_rows(tile):
        return pl.ds(pl.multiple_of(tile * TILE, TILE), TILE)

    own_pieces = modes // PIECE // 2 if shared else modes // PIECE
    first_piece = (group % 2) * own_pieces if shared else 0
    other_piece = own_pieces - first_piece

    def piece_rows(piece):
        return pl.ds(pl.multiple_of(piece * PIECE, PIECE), PIECE)

    def batch_rows(batch):
        return pl.ds(pl.multiple_of(batch * ROWS, ROWS), ROWS)

    def remote(source, target, send_sem, recv_sem, device):
        return pltpu.make_async_remote_copy(
            src_ref=source, dst_ref=target, send_sem=send_sem, recv_sem=recv_sem,
            device_id={"sec": device}, device_id_type=MESH,
        )

    load_t0 = pltpu.make_async_copy(trans_ref.at[0], upper_t, local_sem.at[0])
    load_t1 = pltpu.make_async_copy(trans_ref.at[0], lower_t, local_sem.at[0])
    load_r0 = pltpu.make_async_copy(refl_ref.at[0], upper_r, local_sem.at[1])

    @pl.when(on_zero)
    def _():
        load_t0.start()
        load_r0.start()

    @pl.when(on_one)
    def _():
        load_t1.start()

    barrier = pltpu.get_barrier_semaphore()

    def greet(device):
        pl.semaphore_signal(barrier, inc=1, device_id={"sec": device}, device_id_type=MESH)

    greet(partner)
    zero_odd = jnp.logical_and(on_zero, odd)
    one_even = jnp.logical_and(on_one, even)
    one_odd = jnp.logical_and(jnp.logical_and(on_one, odd), not_last)
    even_paired = jnp.logical_and(one_even, paired)
    even_inside = jnp.logical_and(one_even, not_first)

    @pl.when(zero_odd)
    def _():
        greet(above)

    @pl.when(one_even)
    def _():
        greet(me + 1)
        if shared:
            pl.semaphore_signal(
                barrier, inc=1, device_id={"freq": mate, "sec": me}, device_id_type=MESH
            )

    @pl.when(even_paired)
    def _():
        greet(lax.rem(me + 2, n))
        greet(lax.rem(me + 4, n))

    @pl.when(even_inside)
    def _():
        greet(beside)
        greet(above)

    @pl.when(one_odd)
    def _():
        greet(beside)
        greet(lax.rem(me + 2, n))

    def number(flag):
        return flag.astype(jnp.int32)

    peers = (
        1 + number(zero_odd) + (2 if shared else 1) * number(one_even)
        + 2 * (number(even_paired) + number(even_inside) + number(one_odd))
    )
    pl.semaphore_wait(barrier, peers)

    def tile_copy(tile):
        return remote(
            trans_ref.at[0, tile_rows(tile), :], upper_t.at[tile_rows(tile), :],
            tile_send.at[tile], tile_recv.at[tile], partner,
        )

    share_r = remote(refl_ref.at[0], lower_r, pair_send, pair_recv, partner)

    def down_copy(batch):
        return remote(
            down_out.at[batch_rows(batch), :], down_in.at[batch_rows(batch), :],
            down_send.at[batch], down_recv.at[batch], below,
        )

    def middle_copy(batch):
        return remote(
            down_out.at[batch_rows(batch), :], down_in.at[batch_rows(batch), :],
            down_send.at[batch], down_recv.at[batch], partner,
        )

    def pass_copy(batch):
        return remote(
            down_in.at[batch_rows(batch), :], down_in.at[batch_rows(batch), :],
            pass_send.at[batch], down_recv.at[batch], partner,
        )

    def up_copy(batch):
        return remote(
            up_out.at[batch_rows(batch), :], up_in.at[batch_rows(batch), :],
            up_send.at[batch], up_recv.at[batch], above,
        )

    def side_copy(batch):
        return remote(
            up_out.at[batch_rows(batch), :], up_in.at[batch_rows(batch), :],
            side_send.at[batch], up_recv.at[batch], beside,
        )

    def forward_copy(batch):
        return remote(
            up_in.at[batch_rows(batch), :], up_in.at[batch_rows(batch), :],
            forward_send.at[batch], up_recv.at[batch], lax.rem(me + 2, n),
        )

    def odd_copy(piece):
        rows = piece_rows(piece)
        return remote(
            merged_t.at[rows, :], odd_t.at[rows, :], odd_send.at[piece], odd_recv.at[piece], beside,
        )

    def mate_copy(piece):
        rows = piece_rows(piece)
        return pltpu.make_async_remote_copy(
            src_ref=pair_t.at[rows, :], dst_ref=pair_t.at[rows, :],
            send_sem=mate_send.at[piece], recv_sem=mate_recv.at[piece],
            device_id={"freq": mate, "sec": me}, device_id_type=MESH,
        )

    def piece_copy(piece):
        rows = piece_rows(piece)
        return remote(
            merged.at[rows, :], odd_t.at[rows, :], piece_send.at[piece], piece_recv.at[piece], above,
        )

    def swap_copy(piece):
        rows = piece_rows(piece)
        return pltpu.make_async_remote_copy(
            src_ref=odd_t.at[rows, :], dst_ref=odd_t.at[rows, :],
            send_sem=swap_send.at[piece], recv_sem=swap_recv.at[piece],
            device_id={"freq": mate, "sec": me}, device_id_type=MESH,
        )

    def echo_copy(batch):
        rows = batch_rows(batch)
        return remote(
            echo.at[rows, :], echo.at[rows, :], echo_send.at[batch], echo_recv.at[batch], partner,
        )

    def odd_echo_copy(batch):
        rows = batch_rows(batch)
        return remote(
            odd_out.at[rows, :], odd_echo.at[rows, :],
            odd_echo_send.at[batch], odd_echo_recv.at[batch], above,
        )

    def half_copy(place):
        batch = (1 - parity) * half_batches + place
        return remote(
            up_out.at[batch_rows(batch), :], half_in.at[batch_rows(place), :],
            half_send.at[place], half_recv.at[place], partner,
        )

    def unit_rows():
        count = modes_ref.shape[1]
        row_at = lax.broadcasted_iota(jnp.int32, (count, count), 0)
        col_at = lax.broadcasted_iota(jnp.int32, (count, count), 1)
        spread = jnp.where(row_at == col_at, jnp.broadcast_to(modes_ref[...], (count, count)), 0)
        column = jnp.sum(spread, axis=1, keepdims=True)
        places = lax.broadcasted_iota(jnp.int32, (count, modes), 1)
        return (column == places).astype(F32).astype(BF16)

    def own_half():
        for which in (0, 1):
            @pl.when(parity == which)
            def _():
                out_ref[0] = up_out[which * half:(which + 1) * half, :]

    @pl.when(on_zero)
    def _():
        @pl.when(is_first)
        def _():
            down_in[...] = unit_rows()
            load_t0.wait()

            def go(batch):
                rows = batch_rows(batch)
                down_out[rows, :] = nn(down_in[rows, :], upper_t[...]).astype(BF16)
                middle_copy(batch).start()

            each(batches, go)

        each(tiles, lambda tile: tile_copy(tile).start())

        @pl.when(not_first)
        def _():
            load_t0.wait()

        def turn_tile(tile):
            merged_t[:, tile_rows(tile)] = upper_t[tile_rows(tile), :].T

        each(tiles, turn_tile)
        load_r0.wait()
        share_r.wait_recv()

        def refl_tile(tile):
            rows = tile_rows(tile)
            half_way = nn(upper_t[rows, :], lower_r[...]).astype(BF16)
            merged[rows, :] = (
                upper_r[rows, :].astype(F32) + nn(half_way, merged_t[...])
            ).astype(BF16)

        def own_tile(place):
            tile = first_own + place
            refl_tile(tile)

            @pl.when(is_last)
            def _():
                each(TILE // PIECE, lambda part: piece_copy(tile * (TILE // PIECE) + part).start())

        each(own_tiles, own_tile)
        if shared:
            each(own_tiles, lambda place: refl_tile(first_other + place))

        def reflect(batch):
            rows = batch_rows(batch)

            @pl.when(not_first)
            def _():
                pass_copy(batch).wait_recv()

            value = nn(down_in[rows, :], merged[...])
            up_out[rows, :] = value.astype(BF16)

            @pl.when(not_last)
            def _():
                echo[rows, :] = value
                odd_out[rows, :] = value.astype(BF16)
                echo_copy(batch).start()

                @pl.when(odd)
                def _():
                    odd_echo_copy(batch).start()

            @pl.when(jnp.logical_and(is_last, batch >= half_batches))
            def _():
                half_copy(batch - half_batches).start()

        each(batches, reflect)

        @pl.when(is_last)
        def _():
            own_half()
            each(half_batches, lambda place: half_copy(place).wait_send())
            each(own_pieces, lambda place: piece_copy(first_piece + place).wait_send())

        @pl.when(not_last)
        def _():
            @pl.when(is_first)
            def _():
                each(batches, lambda batch: middle_copy(batch).wait_send())

            each(half_batches, lambda place: half_copy(place).wait_recv())
            out_ref[0] = half_in[...]
            each(batches, lambda batch: echo_copy(batch).wait_send())

            @pl.when(odd)
            def _():
                each(batches, lambda batch: odd_echo_copy(batch).wait_send())

        each(tiles, lambda tile: tile_copy(tile).wait_send())

    @pl.when(on_one)
    def _():
        share_r.start()
        load_t1.wait()

        @pl.when(is_first)
        def _():
            def go(batch):
                rows = batch_rows(batch)
                middle_copy(batch).wait_recv()
                down_out[rows, :] = nn(down_in[rows, :], lower_t[...]).astype(BF16)
                down_copy(batch).start()

            each(batches, go)

        quick = section <= 2

        @pl.when(quick)
        def _():
            def row_tile(tile):
                rows = tile_rows(tile)
                tile_copy(tile).wait_recv()
                merged[rows, :] = nn(upper_t[rows, :], lower_t[...]).astype(BF16)

            each(tiles, row_tile)

        def merge_tile(tile):
            columns = tile_rows(tile)
            block = nn(upper_t[...], lower_t[:, columns]).astype(BF16)
            merged[:, columns] = block
            merged_t[columns, :] = block.T

        def own_merge(place):
            tile = first_own + place
            merge_tile(tile)

            @pl.when(one_odd)
            def _():
                each(TILE // PIECE, lambda part: odd_copy(tile * (TILE // PIECE) + part).start())

        @pl.when(jnp.logical_not(quick))
        def _():
            each(tiles, lambda tile: tile_copy(tile).wait_recv())
            each(own_tiles, own_merge)
            if shared:
                each(own_tiles, lambda place: merge_tile(first_other + place))

        def pair_piece(place):
            piece = first_piece + place
            rows = piece_rows(piece)
            odd_copy(piece).wait_recv()
            pair_t[rows, :] = nn(odd_t[rows, :], merged_t[...]).astype(BF16)
            if shared:
                mate_copy(piece).start()

        early_pieces = own_pieces // 2
        early = section >= 4

        @pl.when(jnp.logical_and(even_paired, early))
        def _():
            each(early_pieces, pair_piece)

        @pl.when(jnp.logical_and(on_one, is_turn))
        def _():
            def swap(place):
                piece = first_piece + place
                piece_copy(piece).wait_recv()
                if shared:
                    swap_copy(piece).start()

            each(own_pieces, swap)

        @pl.when(jnp.logical_and(not_first, not_last))
        def _():
            def go(batch):
                rows = batch_rows(batch)
                down_copy(batch).wait_recv()

                @pl.when(is_turn)
                def _():
                    pass_copy(batch).start()

                down_out[rows, :] = nn(down_in[rows, :], merged[...]).astype(BF16)
                down_copy(batch).start()

                @pl.when(paired)
                def _():
                    pass_copy(batch).start()

                @pl.when(jnp.logical_and(odd, jnp.logical_not(paired)))
                def _():
                    pass_copy(batch).start()

            each(batches, go)

        @pl.when(quick)
        def _():
            def flip_tile(tile):
                columns = tile_rows(tile)
                merged_t[columns, :] = merged[:, columns].T

                @pl.when(one_odd)
                def _():
                    each(TILE // PIECE, lambda part: flip_send(tile * (TILE // PIECE) + part))

            def flip_send(piece):
                mine = jnp.logical_and(piece >= first_piece, piece < first_piece + own_pieces)

                @pl.when(mine)
                def _():
                    odd_copy(piece).start()

            each(tiles, flip_tile)

        @pl.when(not_last)
        def _():
            @pl.when(even_paired)
            def _():
                @pl.when(jnp.logical_not(early))
                def _():
                    each(early_pieces, pair_piece)

                each(own_pieces - early_pieces, lambda place: pair_piece(early_pieces + place))
                each(batches, lambda batch: echo_copy(batch).wait_recv())
                each(batches, lambda batch: odd_echo_copy(batch).wait_recv())
                echo[...] += nn(odd_echo[...], merged_t[...])
                if shared:
                    each(own_pieces, lambda place: mate_copy(other_piece + place).wait_recv())

            @pl.when(is_turn)
            def _():
                if shared:
                    each(own_pieces, lambda place: swap_copy(other_piece + place).wait_recv())
                up_in[...] = nn(down_out[...], odd_t[...]).astype(BF16)

            def climb(step_t):
                def go(batch):
                    rows = batch_rows(batch)

                    @pl.when(jnp.logical_not(even_paired))
                    def _():
                        echo_copy(batch).wait_recv()

                    @pl.when(jnp.logical_not(is_turn))
                    def _():
                        up_copy(batch).wait_recv()

                    @pl.when(jnp.logical_and(even_paired, batch < half_batches))
                    def _():
                        forward_copy(batch).start()

                    up_out[rows, :] = (echo[rows, :] + nn(up_in[rows, :], step_t[...])).astype(BF16)

                    @pl.when(even_inside)
                    def _():
                        up_copy(batch).start()

                    @pl.when(batch < half_batches)
                    def _():
                        half_copy(batch).start()

                each(batches, go)

                @pl.when(even_inside)
                def _():
                    each(half_batches, lambda place: side_copy(half_batches + place).start())

            @pl.when(even_paired)
            def _():
                climb(pair_t)

            @pl.when(is_turn)
            def _():
                climb(merged_t)

            @pl.when(one_odd)
            def _():
                for part in (0, 1):
                    first = part * half_batches
                    rows = slice(part * half, (part + 1) * half)
                    each(half_batches, lambda place: echo_copy(first + place).wait_recv())
                    each(half_batches, lambda place: up_copy(first + place).wait_recv())
                    value = echo[rows, :] + nn(up_in[rows, :], merged_t[...])
                    up_out[rows, :] = value.astype(BF16)
                    if part == 0:
                        each(half_batches, lambda place: half_copy(place).start())

            own_half()
            each(batches, lambda batch: down_copy(batch).wait_send())
            each(half_batches, lambda place: half_copy(place).wait_send())

            @pl.when(not_first)
            def _():
                each(batches, lambda batch: pass_copy(batch).wait_send())

            @pl.when(even_inside)
            def _():
                each(batches, lambda batch: up_copy(batch).wait_send())
                each(half_batches, lambda place: side_copy(half_batches + place).wait_send())

            @pl.when(even_paired)
            def _():
                each(half_batches, lambda batch: forward_copy(batch).wait_send())

            @pl.when(one_odd)
            def _():
                each(own_pieces, lambda place: odd_copy(first_piece + place).wait_send())

            if shared:
                @pl.when(even_paired)
                def _():
                    each(own_pieces, lambda place: mate_copy(first_piece + place).wait_send())

                @pl.when(is_turn)
                def _():
                    each(own_pieces, lambda place: swap_copy(first_piece + place).wait_send())

        @pl.when(is_last)
        def _():
            each(half_batches, lambda place: half_copy(place).wait_recv())
            out_ref[0] = half_in[...]

        share_r.wait_send()


def shards(n, groups, layer_trans, layer_refl, source_modes):
    modes = layer_trans.shape[1]
    count = source_modes.shape[0]
    half = count // 2
    batches = count // ROWS
    square = (modes, modes)
    vmem = pl.BlockSpec(memory_space=pltpu.VMEM)
    anywhere = pl.BlockSpec(memory_space=pl.ANY)
    tiles = pltpu.SemaphoreType.DMA((modes // TILE,))
    pieces = pltpu.SemaphoreType.DMA((modes // PIECE,))
    per_batch = pltpu.SemaphoreType.DMA((batches,))
    per_half = pltpu.SemaphoreType.DMA((batches // 2,))
    return pl.pallas_call(
        functools.partial(kernel, n, groups),
        out_shape=jax.ShapeDtypeStruct((1, half, modes), BF16),
        in_specs=[vmem, anywhere, anywhere],
        out_specs=vmem,
        scratch_shapes=[pltpu.VMEM(square, BF16)] * 8 + [
            pltpu.VMEM((count, modes), BF16),
            pltpu.VMEM((count, modes), BF16),
            pltpu.VMEM((count, modes), BF16),
            pltpu.VMEM((count, modes), BF16),
            pltpu.VMEM((count, modes), BF16),
            pltpu.VMEM((count, modes), BF16),
            pltpu.VMEM((half, modes), BF16),
            pltpu.VMEM((count, modes), F32),
            pltpu.SemaphoreType.DMA((2,)),
            pieces,
            pieces,
            per_batch,
            per_batch,
            pieces,
            pieces,
            pieces,
            pieces,
            pieces,
            pieces,
            per_half,
            per_batch,
            tiles,
            tiles,
            pltpu.SemaphoreType.DMA,
            pltpu.SemaphoreType.DMA,
            per_batch,
            per_batch,
            per_batch,
            per_batch,
            per_batch,
            per_batch,
            per_batch,
            per_half,
            per_half,
        ],
        compiler_params=pltpu.CompilerParams(
            collective_id=0, has_side_effects=True, vmem_limit_bytes=56 * 1024 * 1024
        ),
    )(source_modes.reshape(1, -1), layer_trans, layer_refl)


def solution(mesh):
    return jax.shard_map(
        functools.partial(shards, mesh.shape["sec"], mesh.shape["freq"]),
        mesh=mesh,
        in_specs=(P("sec", None, None), P("sec", None, None), P("freq")),
        out_specs=P(("freq", "sec"), None, None),
        check_vma=False,
    )
```

```python
import functools

import jax
import jax.numpy as jnp
from jax import lax
from jax.experimental import pallas as pl
from jax.experimental.pallas import tpu as pltpu
from jax.sharding import PartitionSpec as P

ROWS = 16
TILE = 256
PIECE = 128
F32 = jnp.float32
BF16 = jnp.bfloat16
MESH = pl.DeviceIdType.MESH


def nn(left, right):
    return jnp.dot(left, right, preferred_element_type=F32)


def each(count, body):
    def step(index, carry):
        body(index)
        return carry

    lax.fori_loop(0, count, step, 0)


def kernel(
    n, groups, modes_ref, trans_ref, refl_ref, out_ref,
    upper_t, lower_t, upper_r, lower_r, merged, merged_t, odd_t, pair_t,
    down_in, down_out, up_in, up_out, odd_out, odd_echo, half_in, echo,
    local_sem, odd_send, odd_recv, odd_echo_send, odd_echo_recv, piece_send, piece_recv, swap_send, swap_recv, mate_send, mate_recv, forward_send, side_send, tile_send, tile_recv, pair_send, pair_recv, echo_send, echo_recv,
    down_send, down_recv, pass_send, up_send, up_recv, half_send, half_recv,
):
    me = lax.axis_index("sec")
    section = me // 2
    parity = me % 2
    partner = me + 1 - 2 * parity
    sections = n // 2
    is_first = section == 0
    is_last = section == sections - 1
    not_first = jnp.logical_not(is_first)
    not_last = jnp.logical_not(is_last)
    on_zero = parity == 0
    on_one = parity == 1
    shared = groups % 2 == 0
    group = lax.axis_index("freq")
    mate = group + 1 - 2 * (group % 2) if shared else group
    even = section % 2 == 0
    odd = section % 2 == 1
    paired = section < sections - 2
    is_turn = section == sections - 2
    below = lax.rem(jnp.where(section == sections - 2, me + 1, me + 2), n)
    above = lax.rem(me + n - 1 - 3 * parity, n)
    beside = lax.rem(me + n - 2, n)
    modes = upper_t.shape[0]
    tiles = modes // TILE
    own_tiles = tiles // 2 if shared else tiles
    first_own = (group % 2) * own_tiles if shared else 0
    first_other = own_tiles - first_own
    batches = down_in.shape[0] // ROWS
    half_batches = batches // 2
    half = half_in.shape[0]

    def tile_rows(tile):
        return pl.ds(pl.multiple_of(tile * TILE, TILE), TILE)

    own_pieces = modes // PIECE // 2 if shared else modes // PIECE
    first_piece = (group % 2) * own_pieces if shared else 0
    other_piece = own_pieces - first_piece

    def piece_rows(piece):
        return pl.ds(pl.multiple_of(piece * PIECE, PIECE), PIECE)

    def batch_rows(batch):
        return pl.ds(pl.multiple_of(batch * ROWS, ROWS), ROWS)

    def remote(source, target, send_sem, recv_sem, device):
        return pltpu.make_async_remote_copy(
            src_ref=source, dst_ref=target, send_sem=send_sem, recv_sem=recv_sem,
            device_id={"sec": device}, device_id_type=MESH,
        )

    load_t0 = pltpu.make_async_copy(trans_ref.at[0], upper_t, local_sem.at[0])
    load_t1 = pltpu.make_async_copy(trans_ref.at[0], lower_t, local_sem.at[0])
    load_r0 = pltpu.make_async_copy(refl_ref.at[0], upper_r, local_sem.at[1])

    @pl.when(on_zero)
    def _():
        load_t0.start()
        load_r0.start()

    @pl.when(on_one)
    def _():
        load_t1.start()

    barrier = pltpu.get_barrier_semaphore()

    def greet(device):
        pl.semaphore_signal(barrier, inc=1, device_id={"sec": device}, device_id_type=MESH)

    greet(partner)
    zero_odd = jnp.logical_and(on_zero, odd)
    one_even = jnp.logical_and(on_one, even)
    one_odd = jnp.logical_and(jnp.logical_and(on_one, odd), not_last)
    even_paired = jnp.logical_and(one_even, paired)
    even_inside = jnp.logical_and(one_even, not_first)

    @pl.when(zero_odd)
    def _():
        greet(above)

    @pl.when(one_even)
    def _():
        greet(me + 1)
        if shared:
            pl.semaphore_signal(
                barrier, inc=1, device_id={"freq": mate, "sec": me}, device_id_type=MESH
            )

    @pl.when(even_paired)
    def _():
        greet(lax.rem(me + 2, n))
        greet(lax.rem(me + 4, n))

    @pl.when(even_inside)
    def _():
        greet(beside)
        greet(above)

    @pl.when(one_odd)
    def _():
        greet(beside)
        greet(lax.rem(me + 2, n))

    def number(flag):
        return flag.astype(jnp.int32)

    peers = (
        1 + number(zero_odd) + (2 if shared else 1) * number(one_even)
        + 2 * (number(even_paired) + number(even_inside) + number(one_odd))
    )
    pl.semaphore_wait(barrier, peers)

    def tile_copy(tile):
        return remote(
            trans_ref.at[0, tile_rows(tile), :], upper_t.at[tile_rows(tile), :],
            tile_send.at[tile], tile_recv.at[tile], partner,
        )

    share_r = remote(refl_ref.at[0], lower_r, pair_send, pair_recv, partner)

    def down_copy(batch):
        return remote(
            down_out.at[batch_rows(batch), :], down_in.at[batch_rows(batch), :],
            down_send.at[batch], down_recv.at[batch], below,
        )

    def middle_copy(batch):
        return remote(
            down_out.at[batch_rows(batch), :], down_in.at[batch_rows(batch), :],
            down_send.at[batch], down_recv.at[batch], partner,
        )

    def pass_copy(batch):
        return remote(
            down_in.at[batch_rows(batch), :], down_in.at[batch_rows(batch), :],
            pass_send.at[batch], down_recv.at[batch], partner,
        )

    def up_copy(batch):
        return remote(
            up_out.at[batch_rows(batch), :], up_in.at[batch_rows(batch), :],
            up_send.at[batch], up_recv.at[batch], above,
        )

    def side_copy(batch):
        return remote(
            up_out.at[batch_rows(batch), :], up_in.at[batch_rows(batch), :],
            side_send.at[batch], up_recv.at[batch], beside,
        )

    def forward_copy(batch):
        return remote(
            up_in.at[batch_rows(batch), :], up_in.at[batch_rows(batch), :],
            forward_send.at[batch], up_recv.at[batch], lax.rem(me + 2, n),
        )

    def odd_copy(piece):
        rows = piece_rows(piece)
        return remote(
            merged_t.at[rows, :], odd_t.at[rows, :], odd_send.at[piece], odd_recv.at[piece], beside,
        )

    def mate_copy(piece):
        rows = piece_rows(piece)
        return pltpu.make_async_remote_copy(
            src_ref=pair_t.at[rows, :], dst_ref=pair_t.at[rows, :],
            send_sem=mate_send.at[piece], recv_sem=mate_recv.at[piece],
            device_id={"freq": mate, "sec": me}, device_id_type=MESH,
        )

    def piece_copy(piece):
        rows = piece_rows(piece)
        return remote(
            merged.at[rows, :], odd_t.at[rows, :], piece_send.at[piece], piece_recv.at[piece], above,
        )

    def swap_copy(piece):
        rows = piece_rows(piece)
        return pltpu.make_async_remote_copy(
            src_ref=odd_t.at[rows, :], dst_ref=odd_t.at[rows, :],
            send_sem=swap_send.at[piece], recv_sem=swap_recv.at[piece],
            device_id={"freq": mate, "sec": me}, device_id_type=MESH,
        )

    def echo_copy(batch):
        rows = batch_rows(batch)
        return remote(
            echo.at[rows, :], echo.at[rows, :], echo_send.at[batch], echo_recv.at[batch], partner,
        )

    def odd_echo_copy(batch):
        rows = batch_rows(batch)
        return remote(
            odd_out.at[rows, :], odd_echo.at[rows, :],
            odd_echo_send.at[batch], odd_echo_recv.at[batch], above,
        )

    def half_copy(place):
        batch = (1 - parity) * half_batches + place
        return remote(
            up_out.at[batch_rows(batch), :], half_in.at[batch_rows(place), :],
            half_send.at[place], half_recv.at[place], partner,
        )

    def unit_rows():
        count = modes_ref.shape[1]
        row_at = lax.broadcasted_iota(jnp.int32, (count, count), 0)
        col_at = lax.broadcasted_iota(jnp.int32, (count, count), 1)
        spread = jnp.where(row_at == col_at, jnp.broadcast_to(modes_ref[...], (count, count)), 0)
        column = jnp.sum(spread, axis=1, keepdims=True)
        places = lax.broadcasted_iota(jnp.int32, (count, modes), 1)
        return (column == places).astype(F32).astype(BF16)

    def own_half():
        for which in (0, 1):
            @pl.when(parity == which)
            def _():
                out_ref[0] = up_out[which * half:(which + 1) * half, :]

    @pl.when(on_zero)
    def _():
        @pl.when(is_first)
        def _():
            down_in[...] = unit_rows()
            load_t0.wait()

            def go(batch):
                rows = batch_rows(batch)
                down_out[rows, :] = nn(down_in[rows, :], upper_t[...]).astype(BF16)
                middle_copy(batch).start()

            each(batches, go)

        each(tiles, lambda tile: tile_copy(tile).start())

        @pl.when(not_first)
        def _():
            load_t0.wait()

        def turn_tile(tile):
            merged_t[:, tile_rows(tile)] = upper_t[tile_rows(tile), :].T

        each(tiles, turn_tile)
        load_r0.wait()
        share_r.wait_recv()

        def refl_tile(tile):
            rows = tile_rows(tile)
            half_way = nn(upper_t[rows, :], lower_r[...]).astype(BF16)
            merged[rows, :] = (
                upper_r[rows, :].astype(F32) + nn(half_way, merged_t[...])
            ).astype(BF16)

        def own_tile(place):
            tile = first_own + place
            refl_tile(tile)

            @pl.when(is_last)
            def _():
                each(TILE // PIECE, lambda part: piece_copy(tile * (TILE // PIECE) + part).start())

        each(own_tiles, own_tile)
        if shared:
            each(own_tiles, lambda place: refl_tile(first_other + place))

        def reflect(batch):
            rows = batch_rows(batch)

            @pl.when(not_first)
            def _():
                pass_copy(batch).wait_recv()

            value = nn(down_in[rows, :], merged[...])
            up_out[rows, :] = value.astype(BF16)

            @pl.when(not_last)
            def _():
                echo[rows, :] = value
                odd_out[rows, :] = value.astype(BF16)
                echo_copy(batch).start()

                @pl.when(odd)
                def _():
                    odd_echo_copy(batch).start()

            @pl.when(jnp.logical_and(is_last, batch >= half_batches))
            def _():
                half_copy(batch - half_batches).start()

        each(batches, reflect)

        @pl.when(is_last)
        def _():
            own_half()
            each(half_batches, lambda place: half_copy(place).wait_send())
            each(own_pieces, lambda place: piece_copy(first_piece + place).wait_send())

        @pl.when(not_last)
        def _():
            @pl.when(is_first)
            def _():
                each(batches, lambda batch: middle_copy(batch).wait_send())

            each(half_batches, lambda place: half_copy(place).wait_recv())
            out_ref[0] = half_in[...]
            each(batches, lambda batch: echo_copy(batch).wait_send())

            @pl.when(odd)
            def _():
                each(batches, lambda batch: odd_echo_copy(batch).wait_send())

        each(tiles, lambda tile: tile_copy(tile).wait_send())

    @pl.when(on_one)
    def _():
        share_r.start()
        load_t1.wait()

        @pl.when(is_first)
        def _():
            def go(batch):
                rows = batch_rows(batch)
                middle_copy(batch).wait_recv()
                down_out[rows, :] = nn(down_in[rows, :], lower_t[...]).astype(BF16)
                down_copy(batch).start()

            each(batches, go)

        quick = section <= 2

        @pl.when(quick)
        def _():
            def row_tile(tile):
                rows = tile_rows(tile)
                tile_copy(tile).wait_recv()
                merged[rows, :] = nn(upper_t[rows, :], lower_t[...]).astype(BF16)

            each(tiles, row_tile)

        def merge_tile(tile):
            columns = tile_rows(tile)
            block = nn(upper_t[...], lower_t[:, columns]).astype(BF16)
            merged[:, columns] = block
            merged_t[columns, :] = block.T

        def own_merge(place):
            tile = first_own + place
            merge_tile(tile)

            @pl.when(one_odd)
            def _():
                each(TILE // PIECE, lambda part: odd_copy(tile * (TILE // PIECE) + part).start())

        @pl.when(jnp.logical_not(quick))
        def _():
            each(tiles, lambda tile: tile_copy(tile).wait_recv())
            each(own_tiles, own_merge)
            if shared:
                each(own_tiles, lambda place: merge_tile(first_other + place))

        def pair_piece(place):
            piece = first_piece + place
            rows = piece_rows(piece)
            odd_copy(piece).wait_recv()
            pair_t[rows, :] = nn(odd_t[rows, :], merged_t[...]).astype(BF16)
            if shared:
                mate_copy(piece).start()

        early_pieces = own_pieces // 2
        early = section >= 4

        @pl.when(jnp.logical_and(even_paired, early))
        def _():
            each(early_pieces, pair_piece)

        @pl.when(jnp.logical_and(on_one, is_turn))
        def _():
            def swap(place):
                piece = first_piece + place
                piece_copy(piece).wait_recv()
                if shared:
                    swap_copy(piece).start()

            each(own_pieces, swap)

        @pl.when(jnp.logical_and(not_first, not_last))
        def _():
            def go(batch):
                rows = batch_rows(batch)
                down_copy(batch).wait_recv()

                @pl.when(is_turn)
                def _():
                    pass_copy(batch).start()

                down_out[rows, :] = nn(down_in[rows, :], merged[...]).astype(BF16)
                down_copy(batch).start()

            each(batches, go)

            @pl.when(jnp.logical_not(is_turn))
            def _():
                each(batches, lambda batch: pass_copy(batch).start())

        @pl.when(quick)
        def _():
            def flip_tile(tile):
                columns = tile_rows(tile)
                merged_t[columns, :] = merged[:, columns].T

                @pl.when(one_odd)
                def _():
                    each(TILE // PIECE, lambda part: flip_send(tile * (TILE // PIECE) + part))

            def flip_send(piece):
                mine = jnp.logical_and(piece >= first_piece, piece < first_piece + own_pieces)

                @pl.when(mine)
                def _():
                    odd_copy(piece).start()

            each(tiles, flip_tile)

        @pl.when(not_last)
        def _():
            @pl.when(even_paired)
            def _():
                @pl.when(jnp.logical_not(early))
                def _():
                    each(early_pieces, pair_piece)

                each(own_pieces - early_pieces, lambda place: pair_piece(early_pieces + place))
                each(batches, lambda batch: echo_copy(batch).wait_recv())
                each(batches, lambda batch: odd_echo_copy(batch).wait_recv())
                echo[...] += nn(odd_echo[...], merged_t[...])
                if shared:
                    each(own_pieces, lambda place: mate_copy(other_piece + place).wait_recv())

            @pl.when(is_turn)
            def _():
                if shared:
                    each(own_pieces, lambda place: swap_copy(other_piece + place).wait_recv())
                up_in[...] = nn(down_out[...], odd_t[...]).astype(BF16)

            def climb(step_t):
                def go(batch):
                    rows = batch_rows(batch)

                    @pl.when(jnp.logical_not(even_paired))
                    def _():
                        echo_copy(batch).wait_recv()

                    @pl.when(jnp.logical_not(is_turn))
                    def _():
                        up_copy(batch).wait_recv()

                    @pl.when(jnp.logical_and(even_paired, batch < half_batches))
                    def _():
                        forward_copy(batch).start()

                    up_out[rows, :] = (echo[rows, :] + nn(up_in[rows, :], step_t[...])).astype(BF16)

                    @pl.when(even_inside)
                    def _():
                        up_copy(batch).start()

                    @pl.when(batch < half_batches)
                    def _():
                        half_copy(batch).start()

                each(batches, go)

                @pl.when(even_inside)
                def _():
                    each(half_batches, lambda place: side_copy(half_batches + place).start())

            @pl.when(even_paired)
            def _():
                climb(pair_t)

            @pl.when(is_turn)
            def _():
                climb(merged_t)

            @pl.when(one_odd)
            def _():
                for part in (0, 1):
                    first = part * half_batches
                    rows = slice(part * half, (part + 1) * half)
                    each(half_batches, lambda place: echo_copy(first + place).wait_recv())
                    each(half_batches, lambda place: up_copy(first + place).wait_recv())
                    value = echo[rows, :] + nn(up_in[rows, :], merged_t[...])
                    up_out[rows, :] = value.astype(BF16)
                    if part == 0:
                        each(half_batches, lambda place: half_copy(place).start())

            own_half()
            each(batches, lambda batch: down_copy(batch).wait_send())
            each(half_batches, lambda place: half_copy(place).wait_send())

            @pl.when(not_first)
            def _():
                each(batches, lambda batch: pass_copy(batch).wait_send())

            @pl.when(even_inside)
            def _():
                each(batches, lambda batch: up_copy(batch).wait_send())
                each(half_batches, lambda place: side_copy(half_batches + place).wait_send())

            @pl.when(even_paired)
            def _():
                each(half_batches, lambda batch: forward_copy(batch).wait_send())

            @pl.when(one_odd)
            def _():
                each(own_pieces, lambda place: odd_copy(first_piece + place).wait_send())

            if shared:
                @pl.when(even_paired)
                def _():
                    each(own_pieces, lambda place: mate_copy(first_piece + place).wait_send())

                @pl.when(is_turn)
                def _():
                    each(own_pieces, lambda place: swap_copy(first_piece + place).wait_send())

        @pl.when(is_last)
        def _():
            each(half_batches, lambda place: half_copy(place).wait_recv())
            out_ref[0] = half_in[...]

        share_r.wait_send()


def shards(n, groups, layer_trans, layer_refl, source_modes):
    modes = layer_trans.shape[1]
    count = source_modes.shape[0]
    half = count // 2
    batches = count // ROWS
    square = (modes, modes)
    vmem = pl.BlockSpec(memory_space=pltpu.VMEM)
    anywhere = pl.BlockSpec(memory_space=pl.ANY)
    tiles = pltpu.SemaphoreType.DMA((modes // TILE,))
    pieces = pltpu.SemaphoreType.DMA((modes // PIECE,))
    per_batch = pltpu.SemaphoreType.DMA((batches,))
    per_half = pltpu.SemaphoreType.DMA((batches // 2,))
    return pl.pallas_call(
        functools.partial(kernel, n, groups),
        out_shape=jax.ShapeDtypeStruct((1, half, modes), BF16),
        in_specs=[vmem, anywhere, anywhere],
        out_specs=vmem,
        scratch_shapes=[pltpu.VMEM(square, BF16)] * 8 + [
            pltpu.VMEM((count, modes), BF16),
            pltpu.VMEM((count, modes), BF16),
            pltpu.VMEM((count, modes), BF16),
            pltpu.VMEM((count, modes), BF16),
            pltpu.VMEM((count, modes), BF16),
            pltpu.VMEM((count, modes), BF16),
            pltpu.VMEM((half, modes), BF16),
            pltpu.VMEM((count, modes), F32),
            pltpu.SemaphoreType.DMA((2,)),
            pieces,
            pieces,
            per_batch,
            per_batch,
            pieces,
            pieces,
            pieces,
            pieces,
            pieces,
            pieces,
            per_half,
            per_batch,
            tiles,
            tiles,
            pltpu.SemaphoreType.DMA,
            pltpu.SemaphoreType.DMA,
            per_batch,
            per_batch,
            per_batch,
            per_batch,
            per_batch,
            per_batch,
            per_batch,
            per_half,
            per_half,
        ],
        compiler_params=pltpu.CompilerParams(
            collective_id=0, has_side_effects=True, vmem_limit_bytes=56 * 1024 * 1024
        ),
    )(source_modes.reshape(1, -1), layer_trans, layer_refl)


def solution(mesh):
    return jax.shard_map(
        functools.partial(shards, mesh.shape["sec"], mesh.shape["freq"]),
        mesh=mesh,
        in_specs=(P("sec", None, None), P("sec", None, None), P("freq")),
        out_specs=P(("freq", "sec"), None, None),
        check_vma=False,
    )
```
